512 devices in a mesh: energy: 64 (over y, x, z_hi), mom: 8 (over z_lo, core).
Axes of the slice: x: 4, y: 8, z: 8 (z_hi: 2, z_lo: 4; z = z_hi * 4 + z_lo), core: 2. Of those that a mesh axis runs over, the one named last changes fastest.
Arguments:
- green_lesser: bfloat16 [384, 32, 64, 128], P('energy', 'mom'), may hold values from -6 to 6
- occupation: float32 [16], replicated, may hold values from 0.05 to 2
- transfer_coupling: bfloat16 [16, 32], replicated, may hold values from -0.5 to 0.5
- orbital_coupling: bfloat16 [16, 2, 64, 64], replicated, may hold values from -0.5 to 0.5
- phonon_offsets: int32 [16], replicated, may hold values from 1 to 2, as said below
- transfer_index: int32 [32, 32], replicated, may hold values from 0 to 31, as said below
Outputs:
- sigma_lesser: float32 [384, 32, 64, 128], P('energy', 'mom')
The draws below stay inside these ranges and needn't reach their ends.
Inputs may be any that keep to these rules, and one draw needn't show every extreme that they name: `phonon_offsets`: some phonon energy equals 2 steps. `transfer_index`: each row names every momentum-transfer index once.
All inputs are finite; a program needn't handle non-finite values.
Results may differ from the reference program's by a relative error of at most 0.0049.
Values may be sent and summed in bfloat16 or wider, within the bound.
A program may use at most 64 MiB of HBM per device.

```python
import math
import jax
import jax.numpy as jnp
from jax import lax

NO = 64
NW = 16
NK = 32
NE = 384
OFFMAX = 2


def draw_phonon_offsets(key, part):
    key = jax.random.fold_in(key, 3)
    first_key, second_key = jax.random.split(key)
    drawn = jax.random.randint(first_key, (NW,), 1, OFFMAX + 1)
    marked = jax.random.randint(second_key, (), 0, NW)
    return jnp.where(jnp.arange(NW) == marked, OFFMAX, drawn).astype(jnp.int32)


def permute_row(row_key):
    return jax.random.permutation(row_key, NK)


def draw_transfer_index(key, part):
    key = jax.random.fold_in(key, 5)
    row_keys = jax.random.split(key, NK)
    return jax.vmap(permute_row)(row_keys).astype(jnp.int32)


def levels(key, shape, cuts, low, high):
    level = 1.0
    for dim, shards_of in cuts:
        steps = jax.random.uniform(jax.random.fold_in(jax.random.fold_in(key, 6), dim), (shards_of,), jnp.float32, low / len(cuts), high / len(cuts))
        level = level * jnp.repeat(jnp.exp(steps), shape[dim] // shards_of).reshape((-1,) + (1,) * (len(shape) - 1 - dim))
    return level


def centred(rng, shape, scale, reach, shards=(), kind=jnp.bfloat16):
    entries = jax.random.normal(rng, shape, jnp.float32) * scale
    if len(shards) > 0:
        entries = levels(rng, shape, shards, -0.22, 0.18) * entries
    return jnp.clip(entries, min=-reach, max=reach).astype(kind)


def setup_inputs(seed: int = 0) -> dict:
    key_list = jax.random.split(jax.random.key(seed), 7)
    green_lesser = centred(key_list[0], (NE, NK, NO, 2 * NO), 1.0, 6.0, ((0, 64), (1, 8)))
    occupation = jnp.clip(jnp.exp(jax.random.uniform(key_list[1], (NW,), jnp.float32, math.log(0.05), math.log(2.0))), 0.05, 2.0)
    transfer_coupling = centred(key_list[2], (NW, NK), (4 * NK) ** -0.5, 0.5)
    orbital_coupling = centred(key_list[3], (NW, 2, NO, NO), (2 * NO) ** -0.5, 0.5)
    phonon_offsets = draw_phonon_offsets(jax.random.fold_in(key_list[6], 71), 0)
    transfer_index = draw_transfer_index(jax.random.fold_in(key_list[6], 71), 0)
    return {"green_lesser": green_lesser, "occupation": occupation, "transfer_coupling": transfer_coupling, "orbital_coupling": orbital_coupling, "phonon_offsets": phonon_offsets, "transfer_index": transfer_index}


def lookup(row_values, table):
    labels = jnp.arange(row_values.shape[0], dtype=jnp.int32)
    picked = (table[:, :, None] == labels[None, None, :]).astype(jnp.float32)
    return jnp.sum(row_values[None, None, :] * picked, axis=-1)


def sandwich(mixed, coupling_pair):
    real_part = coupling_pair[0]
    imag_part = coupling_pair[1]
    half = mixed.shape[-1] // 2
    turned = jnp.concatenate([-mixed[..., half:], mixed[..., :half]], axis=-1)
    stacked = jnp.concatenate([mixed, turned], axis=-2)
    left_side = jnp.concatenate([real_part, imag_part], axis=1)
    right_side = jnp.concatenate([jnp.concatenate([real_part.T, -imag_part.T], axis=1), jnp.concatenate([imag_part.T, real_part.T], axis=1)], axis=0)
    product = jnp.einsum("rs,eksc->ekrc", left_side.astype(jnp.float32), stacked.astype(jnp.float32)).astype(jnp.bfloat16)
    return jnp.einsum("ekrs,sc->ekrc", product.astype(jnp.float32), right_side.astype(jnp.float32))


def reference(green_lesser, occupation, transfer_coupling, orbital_coupling, phonon_offsets, transfer_index):
    energies = green_lesser.shape[0]
    padded = jnp.pad(green_lesser, ((OFFMAX, OFFMAX), (0, 0), (0, 0), (0, 0)))

    def one_mode(mode, total):
        offset = phonon_offsets[mode].astype(jnp.int32)
        lower = lax.dynamic_slice_in_dim(padded, (OFFMAX - offset).astype(jnp.int32), energies, 0)
        upper = lax.dynamic_slice_in_dim(padded, (OFFMAX + offset).astype(jnp.int32), energies, 0)
        spread = lookup(transfer_coupling[mode].astype(jnp.float32), transfer_index)
        weight_low = (occupation[mode] * spread).astype(jnp.bfloat16)
        weight_high = ((occupation[mode] + 1.0) * spread).astype(jnp.bfloat16)
        mixed = jnp.einsum("kq,eqrc->ekrc", weight_low.astype(jnp.float32), lower.astype(jnp.float32))
        mixed = mixed + jnp.einsum("kq,eqrc->ekrc", weight_high.astype(jnp.float32), upper.astype(jnp.float32))
        mixed = mixed.astype(jnp.bfloat16)
        return total + sandwich(mixed, orbital_coupling[mode])

    start = jnp.zeros(green_lesser.shape, jnp.float32)
    return lax.fori_loop(0, NW, one_mode, start)
```

```python
import functools

import jax
import jax.numpy as jnp
from jax import lax
from jax.experimental import pallas as pl
from jax.experimental.pallas import tpu as pltpu
from jax.sharding import PartitionSpec as P

MESH = pl.DeviceIdType.MESH
BF16 = jnp.bfloat16
F32 = jnp.float32

NO = 64
NW = 16
NK = 32
EB = 6
KB = 4
CHIPS = 4
PAIRS = 5
HALF = NO // 2
ROWS = 16
DEPTH = 3 * CHIPS * ROWS
TGT = 2 * KB * NW
RAWSTEP = 40
MIXSTEP = TGT + 8


def up_sends(chip, slot):
    pair, source = slot
    if chip < CHIPS - 1:
        if pair in (1, 2, 3):
            keep = source <= chip
        else:
            keep = source >= 1 + 2 * chip
        return [("up", 0, chip + 1, slot)] if keep else []
    if pair == 3:
        return [("up", 1, 0, (0, source))]
    if pair == 1:
        return [("up", -1, 0, (4, source))]
    return []


def mirror(slot):
    return (slot[0], CHIPS - 1 - slot[1])


def sends(chip, slot):
    out = up_sends(chip, slot)
    for _, step, there, to in up_sends(CHIPS - 1 - chip, mirror(slot)):
        out.append(("down", step, CHIPS - 1 - there, mirror(to)))
    return out


def arrivals():
    queue = {(chip, link): [] for chip in range(CHIPS) for link in ("up", "down")}
    came = {chip: [] for chip in range(CHIPS)}
    for chip in range(CHIPS):
        for pair in (1, 3, 2):
            for link, _, there, to in sends(chip, (pair, chip)):
                queue[chip, link].append((0, there, to))
    for now in range(64):
        landed = []
        for key in queue:
            if queue[key] and queue[key][0][0] <= now:
                _, there, to = queue[key].pop(0)
                landed.append((there, to))
        for there, to in landed:
            came[there].append(to)
            for link, _, further, onward in sends(there, to):
                queue[there, link].append((now + 1, further, onward))
    return came


def flat(slot):
    return slot[0] * CHIPS + slot[1]


def kernel(
    g_ref, occ_ref, off_ref, tc_ref, idx_ref, orb_ref, out_ref,
    raw, spread_rows, buf, weights, left_mats, right_mats, mixed, total,
    own_sem, raw_send, raw_recv, ici_send, ici_recv, sib_send, sib_recv,
):
    energies = lax.axis_size("energy")
    energy = lax.axis_index("energy")
    mom = lax.axis_index("mom")
    core = lax.rem(mom, 2)
    chip = lax.div(mom, 2)
    sibling = (energy, mom + 1 - 2 * core)
    came = arrivals()

    def device(step, there):
        return (lax.rem(energy + step + energies, energies), 2 * there + core)

    def partners(place):
        if place == 0:
            return [(1, CHIPS - 1), (-1, CHIPS - 1), (0, 1)]
        if place == CHIPS - 1:
            return [(1, 0), (-1, 0), (0, CHIPS - 2)]
        return [(0, place - 1), (0, place + 1)]

    def half(slot, side):
        return buf.at[slot[0], slot[1], pl.ds(side * HALF, HALF)]

    own = pltpu.make_async_copy(
        g_ref.at[:, :, pl.ds(core * HALF, HALF)], raw.at[core], own_sem
    )
    own.start()

    barrier = pltpu.get_barrier_semaphore()
    pl.semaphore_signal(barrier, inc=1, device_id=sibling, device_id_type=MESH)
    for place in range(CHIPS):

        @pl.when(chip == place)
        def _(place=place):
            for step, there in partners(place):
                pl.semaphore_signal(
                    barrier, inc=1, device_id=device(step, there), device_id_type=MESH
                )
            pl.semaphore_wait(barrier, 1 + len(partners(place)))

    raw_copy = pltpu.make_async_remote_copy(
        src_ref=g_ref.at[:, :, pl.ds((1 - core) * HALF, HALF)],
        dst_ref=raw.at[core],
        send_sem=raw_send,
        recv_sem=raw_recv,
        device_id=sibling,
        device_id_type=MESH,
    )
    raw_copy.start()
    own.wait()
    pltpu.make_async_remote_copy(
        src_ref=g_ref.at[:, :, pl.ds((1 - core) * HALF, HALF)],
        dst_ref=raw.at[1 - core],
        send_sem=raw_send,
        recv_sem=raw_recv,
        device_id=sibling,
        device_id_type=MESH,
    ).wait_recv()

    for pair in (0, 2, 1):
        for e in range(2):
            for side in range(2):
                for q in range(KB):
                    n = pair * ROWS + e * 8 + side * KB + q
                    spread_rows[pl.ds(n * RAWSTEP, HALF), :] = raw[
                        side, 2 * pair + e, q
                    ].astype(F32)

        def turn(r, carry, pair=pair):
            rows = spread_rows[
                pl.ds(pair * ROWS * RAWSTEP + r, ROWS, stride=RAWSTEP), :
            ]
            buf[pair + 1, chip, core * HALF + r] = rows.astype(BF16)
            return carry

        lax.fori_loop(0, HALF, turn, 0)

    def ici_copy(slot, link, step, there, to):
        return pltpu.make_async_remote_copy(
            src_ref=half(slot, core),
            dst_ref=half(to, core),
            send_sem=ici_send.at[0 if link == "up" else 1, flat(slot)],
            recv_sem=ici_recv.at[flat(to)],
            device_id=device(step, there),
            device_id_type=MESH,
        )

    def sib_copy(slot, side):
        return pltpu.make_async_remote_copy(
            src_ref=half(slot, side),
            dst_ref=half(slot, side),
            send_sem=sib_send.at[flat(slot)],
            recv_sem=sib_recv.at[flat(slot)],
            device_id=sibling,
            device_id_type=MESH,
        )

    for place in range(CHIPS):

        @pl.when(chip == place)
        def _(place=place):
            for pair in (1, 3, 2):
                slot = (pair, place)
                for link, step, there, to in sends(place, slot):
                    ici_copy(slot, link, step, there, to).start()
                sib_copy(slot, core).start()

    column = lax.broadcasted_iota(jnp.int32, (NK, DEPTH), 1)
    source = lax.div(lax.rem(column, CHIPS * ROWS), ROWS) * 8 + lax.rem(column, 8)
    label = lax.broadcasted_iota(jnp.int32, (NK, DEPTH), 0)
    widen = (source == label).astype(F32).astype(BF16)
    target = lax.broadcasted_iota(jnp.int32, (8, NK), 0) + mom * KB
    pick = (target == lax.broadcasted_iota(jnp.int32, (8, NK), 1)).astype(F32).astype(BF16)
    table = idx_ref[...].astype(F32).astype(BF16)
    table = jnp.dot(pick, table, preferred_element_type=F32).astype(BF16)
    table = jnp.dot(table, widen, preferred_element_type=F32)
    mode = lax.broadcasted_iota(jnp.int32, (NW, DEPTH), 0)
    occ = jnp.zeros((NW, DEPTH), F32)
    off = jnp.zeros((NW, DEPTH), jnp.int32)
    for w in range(NW):
        occ = jnp.where(mode == w, occ_ref[w], occ)
        off = jnp.where(mode == w, off_ref[w], off)
    place_of = lax.broadcasted_iota(jnp.int32, (NW, DEPTH), 1)
    pair_of = lax.div(place_of, CHIPS * ROWS)
    energy_of = 2 * (pair_of - 1) + lax.div(lax.rem(place_of, ROWS), 8)
    first = (energy > 0).astype(F32)
    last = (energy < energies - 1).astype(F32)
    for k in range(KB):
        chosen = (table[k : k + 1, :] == label.astype(F32)).astype(F32).astype(BF16)
        spread = jnp.dot(tc_ref[...], chosen, preferred_element_type=F32)
        low = (occ * spread).astype(BF16).astype(F32)
        high = ((occ + 1.0) * spread).astype(BF16).astype(F32)
        for e in range(2):
            away = energy_of - e
            value = jnp.where(away < 0, low, high)
            value = jnp.where(jnp.abs(away) == off, value, 0.0)
            rows = pl.ds((e * KB + k) * NW, NW)
            weights[1, rows, :] = value.astype(BF16)
            weights[0, rows, :] = jnp.where(pair_of == 0, value * first, value).astype(BF16)
            weights[2, rows, :] = jnp.where(pair_of == 2, value * last, value).astype(BF16)

    for w in range(NW):
        real = orb_ref[w, 0].astype(F32)
        imag = orb_ref[w, 1].astype(F32)
        top = jnp.concatenate([real, imag], axis=1)
        bottom = jnp.concatenate([-imag, real], axis=1)
        left_mats[w] = top.astype(BF16)
        right_mats[pl.ds(w * 128, 128), :] = jnp.concatenate([top, bottom], axis=0).T.astype(BF16)

    for place in range(CHIPS):

        @pl.when(chip == place)
        def _(place=place):
            for slot in came[place]:
                ici_copy(slot, "up", 0, 0, slot).wait_recv()
                for link, step, there, to in sends(place, slot):
                    ici_copy(slot, link, step, there, to).start()
                sib_copy(slot, core).start()
            for pair in (1, 3, 2):
                sib_copy((pair, place), 1 - core).wait_recv()
            for slot in came[place]:
                sib_copy(slot, 1 - core).wait_recv()

    def block(t, carry):
        def mix(i, carry):
            wide = []
            for r in (2 * i, 2 * i + 1):
                parts = [
                    buf[t + p, s, r] for p in range(3) for s in range(CHIPS)
                ]
                wide.append(jnp.concatenate(parts, axis=0))
            got = jnp.dot(
                weights[t], jnp.concatenate(wide, axis=1), preferred_element_type=F32
            )
            mixed[pl.ds(pl.multiple_of(2 * i * MIXSTEP, 8), TGT), :] = got[:, :128]
            mixed[pl.ds(pl.multiple_of((2 * i + 1) * MIXSTEP, 8), TGT), :] = got[:, 128:]
            return carry

        lax.fori_loop(0, HALF, mix, 0)
        total[...] = jnp.zeros_like(total)

        def modes(i, carry):
            lefts = []
            for w in (2 * i, 2 * i + 1):
                rows = []
                for j in range(KB):
                    stacked = []
                    for n in (2 * j, 2 * j + 1):
                        m = mixed[pl.ds(n * NW + w, NO, stride=MIXSTEP), :]
                        turned = jnp.concatenate([-m[:, NO:], m[:, :NO]], axis=1)
                        stacked.append(jnp.concatenate([m, turned], axis=0))
                    both = jnp.concatenate(stacked, axis=1).astype(BF16)
                    got = jnp.dot(left_mats[w], both, preferred_element_type=F32)
                    rows += [got[:, :128], got[:, 128:]]
                lefts.append(jnp.concatenate(rows, axis=0).astype(BF16))
            right = right_mats[pl.ds(pl.multiple_of(i * 256, 256), 256), :]
            total[...] += jnp.dot(
                jnp.concatenate(lefts, axis=1), right, preferred_element_type=F32
            )
            return carry

        lax.fori_loop(0, NW // 2, modes, 0)
        for e in range(2):
            for k in range(KB):
                out_ref[2 * t + e, k] = total[pl.ds((e * KB + k) * NO, NO), :]
        return carry

    lax.fori_loop(0, 3, block, 0)

    raw_copy.wait_send()
    for place in range(CHIPS):

        @pl.when(chip == place)
        def _(place=place):
            for slot in [(pair, place) for pair in (1, 3, 2)] + came[place]:
                for link, step, there, to in sends(place, slot):
                    ici_copy(slot, link, step, there, to).wait_send()
                sib_copy(slot, core).wait_send()


def body(green, occupation, coupling, orbital, offsets, index):
    vmem = pl.BlockSpec(memory_space=pltpu.VMEM)
    smem = pl.BlockSpec(memory_space=pltpu.SMEM)
    hbm = pl.BlockSpec(memory_space=pl.ANY)
    slots = PAIRS * CHIPS
    return pl.pallas_call(
        kernel,
        out_shape=jax.ShapeDtypeStruct(green.shape, F32),
        in_specs=[hbm, smem, smem, vmem, vmem, vmem],
        out_specs=vmem,
        scratch_shapes=[
            pltpu.VMEM((2, EB, KB, HALF, 128), BF16),
            pltpu.VMEM((3 * ROWS * RAWSTEP, 128), F32),
            pltpu.VMEM((PAIRS, CHIPS, NO, ROWS, 128), BF16),
            pltpu.VMEM((3, TGT, DEPTH), BF16),
            pltpu.VMEM((NW, NO, 128), BF16),
            pltpu.VMEM((NW * 128, 128), BF16),
            pltpu.VMEM((NO * MIXSTEP, 128), F32),
            pltpu.VMEM((2 * KB * NO, 128), F32),
            pltpu.SemaphoreType.DMA,
            pltpu.SemaphoreType.DMA,
            pltpu.SemaphoreType.DMA,
            pltpu.SemaphoreType.DMA((2, slots)),
            pltpu.SemaphoreType.DMA((slots,)),
            pltpu.SemaphoreType.DMA((slots,)),
            pltpu.SemaphoreType.DMA((slots,)),
        ],
        compiler_params=pltpu.CompilerParams(
            collective_id=0, has_side_effects=True, vmem_limit_bytes=48 * 1024 * 1024
        ),
    )(green, occupation, offsets, coupling, index, orbital)


def solution(mesh):
    placed = (P("energy", "mom", None, None), P(), P(), P(), P(), P())
    return jax.shard_map(
        body, mesh=mesh, in_specs=placed, out_specs=P("energy", "mom", None, None), check_vma=False
    )
```

```python
import jax
import jax.numpy as jnp
from jax import lax
from jax.experimental import pallas as pl
from jax.experimental.pallas import tpu as pltpu
from jax.sharding import PartitionSpec as P

MESH = pl.DeviceIdType.MESH
BF16 = jnp.bfloat16
F32 = jnp.float32

NO = 64
NW = 16
NK = 32
EB = 6
KB = 4
CHIPS = 4
PAIRS = 5
HALF = NO // 2
CHUNK = HALF // 2
ROWS = 16
DEPTH = 3 * CHIPS * ROWS
TGT = 2 * KB * NW
OUT = 2 * KB * NO
RAWSTEP = 40
MIXSTEP = TGT + 8
LINKS = ("up", "down")

UP = (
    (
        (1, 0, 0), (1, 0, 1), (3, 0, 0), (3, 0, 1), (4, 3, 0), (4, 3, 1), (2, 0, 0), (2, 0, 1),
        (4, 2, 0), (4, 2, 1), (0, 3, 0), (0, 3, 1), (4, 1, 0), (4, 1, 1), (0, 1, 0), (0, 1, 1),
        (0, 2, 0), (0, 2, 1),
    ),
    (
        (1, 1, 0), (1, 1, 1), (3, 1, 0), (3, 1, 1), (1, 0, 0), (1, 0, 1), (3, 0, 0), (3, 0, 1),
        (4, 3, 0), (4, 3, 1), (2, 0, 0), (2, 0, 1), (2, 1, 0), (2, 1, 1), (0, 3, 0), (0, 3, 1),
    ),
    (
        (1, 2, 0), (1, 2, 1), (3, 2, 0), (3, 2, 1), (1, 1, 0), (1, 1, 1), (3, 1, 0), (3, 1, 1),
        (1, 0, 0), (1, 0, 1), (3, 0, 0), (3, 0, 1), (2, 2, 0), (2, 2, 1), (2, 0, 0), (2, 0, 1),
        (2, 1, 0), (2, 1, 1),
    ),
    (
        (1, 3, 0), (1, 3, 1), (3, 3, 0), (3, 3, 1), (1, 2, 0), (1, 2, 1), (3, 2, 0), (3, 2, 1),
        (1, 1, 0), (1, 1, 1), (3, 1, 0), (3, 1, 1), (1, 0, 0), (1, 0, 1), (3, 0, 0), (3, 0, 1),
    ),
)
CAP = 3
LAG = 3
STEPS = max(len(row) for row in UP)


def up_target(chip, slot):
    pair, source = slot
    if chip < CHIPS - 1:
        return 0, chip + 1, slot
    return (1, 0, (0, source)) if pair == 3 else (-1, 0, (4, source))


def plan():
    out = [[[] for _ in range(STEPS)] for _ in range(CHIPS)]
    into = [[[] for _ in range(STEPS)] for _ in range(CHIPS)]
    for chip in range(CHIPS):
        for now, entry in enumerate(UP[chip]):
            if not entry:
                continue
            slot, chunk = entry[:2], entry[2]
            step, there, to = up_target(chip, slot)
            out[chip][now].append(("up", step, there, slot, to, chunk))
            into[there][now].append((to, chunk))
            far = [(PAIRS - 1 - s[0], CHIPS - 1 - s[1]) for s in (slot, to)]
            here, there = CHIPS - 1 - chip, CHIPS - 1 - there
            out[here][now].append(("down", -step, there, far[0], far[1], chunk))
            into[there][now].append((far[1], chunk))
    return out, into


def kernel(
    g_ref, occ_hbm, off_hbm, tc_hbm, idx_hbm, orb_hbm, out_ref,
    raw, spread_rows, buf, weights, left_mats, right_mats, mixed, stage,
    occ_ref, off_ref, tc_ref, idx_ref, orb_ref,
    small_sem, own_sem, raw_send, raw_recv, ici_send, ici_recv, sib_send, sib_recv, out_sem,
):
    energies = lax.axis_size("energy")
    energy = lax.axis_index("energy")
    mom = lax.axis_index("mom")
    core = lax.rem(mom, 2)
    chip = lax.div(mom, 2)
    sibling = (energy, mom + 1 - 2 * core)
    outgoing, incoming = plan()
    arrived = [{s: now for now, row in enumerate(rows) for s in row} for rows in incoming]

    def when_complete(place, t):
        slots = [(t + p, s) for p in range(3) for s in range(CHIPS)]
        return max(arrived[place].get((s, c), -1) for s in slots for c in range(2))

    order = [sorted(range(3), key=lambda t, i=i: (when_complete(i, t), t)) for i in range(CHIPS)]
    head = max(when_complete(i, order[i][0]) for i in range(CHIPS)) + 2

    def by_chip(values):
        return sum(jnp.where(chip == i, v, 0) for i, v in enumerate(values))

    def device(step, there):
        return (lax.rem(energy + step + energies, energies), 2 * there + core)

    def partners(place):
        if place == 0:
            return [(1, CHIPS - 1), (-1, CHIPS - 1), (0, 1)]
        if place == CHIPS - 1:
            return [(1, 0), (-1, 0), (0, CHIPS - 2)]
        return [(0, place - 1), (0, place + 1)]

    def on_each_chip(act):
        for place in range(CHIPS):

            @pl.when(chip == place)
            def _(place=place):
                act(place)

    own = pltpu.make_async_copy(
        g_ref.at[:, :, pl.ds(core * HALF, HALF)], raw.at[core], own_sem
    )
    own.start()
    barrier = pltpu.get_barrier_semaphore()
    pl.semaphore_signal(barrier, inc=1, device_id=sibling, device_id_type=MESH)

    def greet(place):
        for step, there in partners(place):
            pl.semaphore_signal(
                barrier, inc=1, device_id=device(step, there), device_id_type=MESH
            )

    on_each_chip(greet)
    small = [
        pltpu.make_async_copy(a, b, small_sem.at[i])
        for i, (a, b) in enumerate(
            [
                (occ_hbm, occ_ref), (off_hbm, off_ref), (tc_hbm, tc_ref),
                (idx_hbm, idx_ref), (orb_hbm, orb_ref),
            ]
        )
    ]
    for copy in small:
        copy.start()
    on_each_chip(lambda place: pl.semaphore_wait(barrier, 1 + len(partners(place))))

    def raw_copy(side):
        return pltpu.make_async_remote_copy(
            src_ref=g_ref.at[:, :, pl.ds((1 - core) * HALF, HALF)],
            dst_ref=raw.at[side],
            send_sem=raw_send,
            recv_sem=raw_recv,
            device_id=sibling,
            device_id_type=MESH,
        )

    raw_copy(core).start()
    own.wait()
    raw_copy(1 - core).wait_recv()

    for pair in range(3):
        for e in range(2):
            for side in range(2):
                for q in range(KB):
                    n = pair * ROWS + e * 8 + side * KB + q
                    spread_rows[pl.ds(n * RAWSTEP, HALF), :] = raw[
                        side, 2 * pair + e, q
                    ].astype(F32)

    def turn(r, carry):
        for pair in range(3):
            rows = spread_rows[
                pl.ds(pair * ROWS * RAWSTEP + r, ROWS, stride=RAWSTEP), :
            ]
            buf[pair + 1, chip, core * HALF + r] = rows.astype(BF16)
        return carry

    lax.fori_loop(0, HALF, turn, 0, unroll=8)

    def rows_of(slot, side, chunk):
        return buf.at[slot[0], slot[1], pl.ds(side * HALF + chunk * CHUNK, CHUNK)]

    def number(slot, chunk):
        return (slot[0] * CHIPS + slot[1]) * 2 + chunk

    def ici_copy(now, link, step, there, slot, to, chunk):
        return pltpu.make_async_remote_copy(
            src_ref=rows_of(slot, core, chunk),
            dst_ref=rows_of(to, core, chunk),
            send_sem=ici_send.at[LINKS.index(link), now % CAP],
            recv_sem=ici_recv.at[number(to, chunk)],
            device_id=device(step, there),
            device_id_type=MESH,
        )

    def sib_copy(slot, chunk, side):
        return pltpu.make_async_remote_copy(
            src_ref=rows_of(slot, side, chunk),
            dst_ref=rows_of(slot, side, chunk),
            send_sem=sib_send.at[number(slot, chunk)],
            recv_sem=sib_recv.at[number(slot, chunk)],
            device_id=sibling,
            device_id_type=MESH,
        )

    got = [set() for _ in range(CHIPS)]

    def receive(place, chunks):
        for slot, chunk in chunks:
            if (slot, chunk) not in got[place]:
                got[place].add((slot, chunk))
                ici_copy(0, "up", 0, 0, slot, slot, chunk).wait_recv()
                sib_copy(slot, chunk, core).start()

    def steps(first, last):
        def act(place):
            for now in range(first, last):
                if CAP <= now < STEPS + CAP:
                    for copy in outgoing[place][now - CAP]:
                        ici_copy(now - CAP, *copy).wait_send()
                if now < STEPS:
                    for copy in outgoing[place][now]:
                        slot, chunk = copy[3], copy[5]
                        if slot[1] != place or slot[0] in (0, 4):
                            receive(place, [(slot, chunk)])
                        ici_copy(now, *copy).start()
                if now == 0:
                    for pair in (1, 2, 3):
                        for chunk in range(2):
                            sib_copy((pair, place), chunk, core).start()
                if LAG <= now < STEPS + LAG:
                    receive(place, incoming[place][now - LAG])

        on_each_chip(act)

    waited = [set() for _ in range(CHIPS)]

    def from_sibling(which):
        def act(place):
            for t in which(place):
                for slot in [(t + p, s) for p in range(3) for s in range(CHIPS)]:
                    if slot not in waited[place]:
                        waited[place].add(slot)
                        for chunk in range(2):
                            sib_copy(slot, chunk, 1 - core).wait_recv()

        on_each_chip(act)

    steps(0, 2)
    for copy in small:
        copy.wait()

    column = lax.broadcasted_iota(jnp.int32, (NK, DEPTH), 1)
    source = lax.div(lax.rem(column, CHIPS * ROWS), ROWS) * 8 + lax.rem(column, 8)
    label = lax.broadcasted_iota(jnp.int32, (NK, DEPTH), 0)
    widen = (source == label).astype(F32).astype(BF16)
    target = lax.broadcasted_iota(jnp.int32, (8, NK), 0) + mom * KB
    pick = (target == lax.broadcasted_iota(jnp.int32, (8, NK), 1)).astype(F32).astype(BF16)
    table = idx_ref[...].astype(F32).astype(BF16)
    table = jnp.dot(pick, table, preferred_element_type=F32).astype(BF16)
    table = jnp.dot(table, widen, preferred_element_type=F32)
    mode = lax.broadcasted_iota(jnp.int32, (NW, DEPTH), 0)
    occ = jnp.zeros((NW, DEPTH), F32)
    off = jnp.zeros((NW, DEPTH), jnp.int32)
    for w in range(NW):
        occ = jnp.where(mode == w, occ_ref[w], occ)
        off = jnp.where(mode == w, off_ref[w], off)
    place_of = lax.broadcasted_iota(jnp.int32, (NW, DEPTH), 1)
    pair_of = lax.div(place_of, CHIPS * ROWS)
    energy_of = 2 * (pair_of - 1) + lax.div(lax.rem(place_of, ROWS), 8)
    first = (energy > 0).astype(F32)
    last = (energy < energies - 1).astype(F32)
    for k in range(KB):
        chosen = (table[k : k + 1, :] == label.astype(F32)).astype(F32).astype(BF16)
        spread = jnp.dot(tc_ref[...], chosen, preferred_element_type=F32)
        low = (occ * spread).astype(BF16).astype(F32)
        high = ((occ + 1.0) * spread).astype(BF16).astype(F32)
        for e in range(2):
            away = energy_of - e
            value = jnp.where(away < 0, low, high)
            value = jnp.where(jnp.abs(away) == off, value, 0.0)
            rows = pl.ds((e * KB + k) * NW, NW)
            weights[1, rows, :] = value.astype(BF16)
            weights[0, rows, :] = jnp.where(pair_of == 0, value * first, value).astype(BF16)
            weights[2, rows, :] = jnp.where(pair_of == 2, value * last, value).astype(BF16)

    for w in range(NW):
        real = orb_ref[w, 0].astype(F32)
        imag = orb_ref[w, 1].astype(F32)
        top = jnp.concatenate([real, imag], axis=1)
        bottom = jnp.concatenate([-imag, real], axis=1)
        left_mats[w] = top.astype(BF16)
        right_mats[pl.ds(w * 128, 128), :] = jnp.concatenate([top, bottom], axis=0).T.astype(BF16)

    def mix(t, first, last):
        def one(i, carry):
            wide = []
            for r in (2 * i, 2 * i + 1):
                parts = [buf[t + p, s, r] for p in range(3) for s in range(CHIPS)]
                wide.append(jnp.concatenate(parts, axis=0))
            got = jnp.dot(
                weights[t], jnp.concatenate(wide, axis=1), preferred_element_type=F32
            )
            mixed[pl.ds(pl.multiple_of(2 * i * MIXSTEP, 8), TGT), :] = got[:, :128]
            mixed[pl.ds(pl.multiple_of((2 * i + 1) * MIXSTEP, 8), TGT), :] = got[:, 128:]
            return carry

        lax.fori_loop(first // 2, last // 2, one, 0, unroll=8)

    def modes(t, first, last):
        rows_out = pl.ds(pl.multiple_of(t * OUT, OUT), OUT)

        def one(i, carry):
            lefts = []
            for w in (2 * i, 2 * i + 1):
                rows = []
                for j in range(KB):
                    stacked = []
                    for n in (2 * j, 2 * j + 1):
                        m = mixed[pl.ds(n * NW + w, NO, stride=MIXSTEP), :]
                        turned = jnp.concatenate([-m[:, NO:], m[:, :NO]], axis=1)
                        stacked.append(jnp.concatenate([m, turned], axis=0))
                    both = jnp.concatenate(stacked, axis=1).astype(BF16)
                    got = jnp.dot(left_mats[w], both, preferred_element_type=F32)
                    rows += [got[:, :128], got[:, 128:]]
                lefts.append(jnp.concatenate(rows, axis=0).astype(BF16))
            right = right_mats[pl.ds(pl.multiple_of(i * 256, 256), 256), :]
            stage[rows_out, :] += jnp.dot(
                jnp.concatenate(lefts, axis=1), right, preferred_element_type=F32
            )
            return carry

        if first == 0:
            stage[rows_out, :] = jnp.zeros((OUT, 128), F32)
        lax.fori_loop(first // 2, last // 2, one, 0, unroll=(last - first) // 2)

    def out_copy(i, t):
        rows = pl.ds(pl.multiple_of(t * OUT, OUT), OUT)
        return pltpu.make_async_copy(stage.at[rows], out_ref.at[rows], out_sem.at[i])

    def first_needs(place):
        t = order[place][0]
        receive(place, [c for row in incoming[place] for c in row if t <= c[0][0] <= t + 2])

    steps(2, head)
    on_each_chip(first_needs)
    steps(head, head + 1)
    from_sibling(lambda place: order[place][:1])
    t = by_chip([o[0] for o in order])
    mix(t, 0, NO // 2)
    steps(head + 1, head + 2)
    mix(t, NO // 2, NO)
    steps(head + 2, head + 3)
    modes(t, 0, NW // 2)
    steps(head + 3, head + 4)
    modes(t, NW // 2, NW)
    out_copy(0, t).start()
    steps(head + 4, STEPS + max(CAP, LAG))
    from_sibling(lambda place: order[place][1:])

    def later(i, carry):
        t = jnp.where(i == 1, by_chip([o[1] for o in order]), by_chip([o[2] for o in order]))
        mix(t, 0, NO)
        modes(t, 0, NW)
        out_copy(i, t).start()
        return carry

    lax.fori_loop(1, 3, later, 0)
    for i in range(3):
        out_copy(i, by_chip([o[i] for o in order])).wait()

    raw_copy(core).wait_send()

    def finish(place):
        for slot in [(p, s) for p in range(PAIRS) for s in range(CHIPS)]:
            for chunk in range(2):
                sib_copy(slot, chunk, core).wait_send()

    finish(0)


def body(green, occupation, coupling, orbital, offsets, index):
    hbm = pl.BlockSpec(memory_space=pltpu.HBM)
    slots = PAIRS * CHIPS * 2
    rows = 3 * OUT
    result = pl.pallas_call(
        kernel,
        out_shape=jax.ShapeDtypeStruct((rows, 128), F32),
        in_specs=[hbm] * 6,
        out_specs=hbm,
        scratch_shapes=[
            pltpu.VMEM((2, EB, KB, HALF, 128), BF16),
            pltpu.VMEM((3 * ROWS * RAWSTEP, 128), F32),
            pltpu.VMEM((PAIRS, CHIPS, NO, ROWS, 128), BF16),
            pltpu.VMEM((3, TGT, DEPTH), BF16),
            pltpu.VMEM((NW, NO, 128), BF16),
            pltpu.VMEM((NW * 128, 128), BF16),
            pltpu.VMEM((NO * MIXSTEP, 128), F32),
            pltpu.VMEM((rows, 128), F32),
            pltpu.SMEM((NW,), F32),
            pltpu.SMEM((NW,), jnp.int32),
            pltpu.VMEM((NW, NK), BF16),
            pltpu.VMEM((NK, NK), jnp.int32),
            pltpu.VMEM((NW, 2, NO, NO), BF16),
            pltpu.SemaphoreType.DMA((5,)),
            pltpu.SemaphoreType.DMA,
            pltpu.SemaphoreType.DMA,
            pltpu.SemaphoreType.DMA,
            pltpu.SemaphoreType.DMA((2, CAP)),
            pltpu.SemaphoreType.DMA((slots,)),
            pltpu.SemaphoreType.DMA((slots,)),
            pltpu.SemaphoreType.DMA((slots,)),
            pltpu.SemaphoreType.DMA((3,)),
        ],
        compiler_params=pltpu.CompilerParams(
            collective_id=0, has_side_effects=True, vmem_limit_bytes=56 * 1024 * 1024
        ),
    )(green, occupation, offsets, coupling, index, orbital)
    return result.reshape(green.shape)


def solution(mesh):
    placed = (P("energy", "mom", None, None), P(), P(), P(), P(), P())
    return jax.shard_map(
        body, mesh=mesh, in_specs=placed, out_specs=P("energy", "mom", None, None), check_vma=False
    )
```

```python
import jax
import jax.numpy as jnp
from jax import lax
from jax.experimental import pallas as pl
from jax.experimental.pallas import tpu as pltpu
from jax.sharding import PartitionSpec as P

MESH = pl.DeviceIdType.MESH
BF16 = jnp.bfloat16
F32 = jnp.float32

NO = 64
NW = 16
NK = 32
EB = 6
KB = 4
CHIPS = 4
PAIRS = 5
HALF = NO // 2
CHUNK = HALF // 2
ROWS = 16
DEPTH = 3 * CHIPS * ROWS
TGT = 2 * KB * NW
OUT = 2 * KB * NO
RAWSTEP = 40
SHIFT = 4
ODD = TGT + 16
MIXSTEP = TGT + 8 + SHIFT
LINKS = ("up", "down")

UP = (
    (
        (1, 0, 0), (1, 0, 1), (3, 0, 0), (3, 0, 1), (4, 3, 0), (4, 3, 1), (2, 0, 0), (2, 0, 1),
        (4, 2, 0), (4, 2, 1), (0, 3, 0), (0, 3, 1), (4, 1, 0), (4, 1, 1), (0, 1, 0), (0, 1, 1),
        (0, 2, 0), (0, 2, 1),
    ),
    (
        (1, 1, 0), (1, 1, 1), (3, 1, 0), (3, 1, 1), (1, 0, 0), (1, 0, 1), (3, 0, 0), (3, 0, 1),
        (4, 3, 0), (4, 3, 1), (2, 0, 0), (2, 0, 1), (2, 1, 0), (2, 1, 1), (0, 3, 0), (0, 3, 1),
    ),
    (
        (1, 2, 0), (1, 2, 1), (3, 2, 0), (3, 2, 1), (1, 1, 0), (1, 1, 1), (3, 1, 0), (3, 1, 1),
        (1, 0, 0), (1, 0, 1), (3, 0, 0), (3, 0, 1), (2, 2, 0), (2, 2, 1), (2, 0, 0), (2, 0, 1),
        (2, 1, 0), (2, 1, 1),
    ),
    (
        (1, 3, 0), (1, 3, 1), (3, 3, 0), (3, 3, 1), (1, 2, 0), (1, 2, 1), (3, 2, 0), (3, 2, 1),
        (1, 1, 0), (1, 1, 1), (3, 1, 0), (3, 1, 1), (1, 0, 0), (1, 0, 1), (3, 0, 0), (3, 0, 1),
    ),
)
CAP = 4
LAG = 3
STEPS = max(len(row) for row in UP)


def up_target(chip, slot):
    pair, source = slot
    if chip < CHIPS - 1:
        return 0, chip + 1, slot
    return (1, 0, (0, source)) if pair == 3 else (-1, 0, (4, source))


def plan():
    out = [[[] for _ in range(STEPS)] for _ in range(CHIPS)]
    into = [[[] for _ in range(STEPS)] for _ in range(CHIPS)]
    for chip in range(CHIPS):
        for now, entry in enumerate(UP[chip]):
            if not entry:
                continue
            slot, chunk = entry[:2], entry[2]
            step, there, to = up_target(chip, slot)
            out[chip][now].append(("up", step, there, slot, to, chunk))
            into[there][now].append((to, chunk))
            far = [(PAIRS - 1 - s[0], CHIPS - 1 - s[1]) for s in (slot, to)]
            here, there = CHIPS - 1 - chip, CHIPS - 1 - there
            out[here][now].append(("down", -step, there, far[0], far[1], chunk))
            into[there][now].append((far[1], chunk))
    return out, into


def kernel(
    g_ref, occ_hbm, off_hbm, tc_hbm, idx_hbm, orb_hbm, out_ref,
    raw, spread_rows, buf, weights, odd_weights, left_mats, right_mats, mixed, stage,
    occ_ref, off_ref, tc_ref, idx_ref, orb_ref,
    small_sem, own_sem, raw_send, raw_recv, ici_send, ici_recv, sib_send, sib_recv, out_sem,
):
    energies = lax.axis_size("energy")
    energy = lax.axis_index("energy")
    mom = lax.axis_index("mom")
    core = lax.rem(mom, 2)
    chip = lax.div(mom, 2)
    sibling = (energy, mom + 1 - 2 * core)
    outgoing, incoming = plan()
    arrived = [{s: now for now, row in enumerate(rows) for s in row} for rows in incoming]

    def when_complete(place, t):
        slots = [(t + p, s) for p in range(3) for s in range(CHIPS)]
        return max(arrived[place].get((s, c), -1) for s in slots for c in range(2))

    order = [sorted(range(3), key=lambda t, i=i: (when_complete(i, t), t)) for i in range(CHIPS)]
    head = max(when_complete(i, order[i][0]) for i in range(CHIPS)) + 3

    def by_chip(values):
        return sum(jnp.where(chip == i, v, 0) for i, v in enumerate(values))

    def device(step, there):
        return (lax.rem(energy + step + energies, energies), 2 * there + core)

    def partners(place):
        if place == 0:
            return [(1, CHIPS - 1), (-1, CHIPS - 1), (0, 1)]
        if place == CHIPS - 1:
            return [(1, 0), (-1, 0), (0, CHIPS - 2)]
        return [(0, place - 1), (0, place + 1)]

    def on_each_chip(act):
        for place in range(CHIPS):

            @pl.when(chip == place)
            def _(place=place):
                act(place)

    own = pltpu.make_async_copy(
        g_ref.at[:, :, pl.ds(core * HALF, HALF)], raw.at[core], own_sem
    )
    own.start()
    barrier = pltpu.get_barrier_semaphore()
    pl.semaphore_signal(barrier, inc=1, device_id=sibling, device_id_type=MESH)

    def greet(place):
        for step, there in partners(place):
            pl.semaphore_signal(
                barrier, inc=1, device_id=device(step, there), device_id_type=MESH
            )

    on_each_chip(greet)
    small = [
        pltpu.make_async_copy(a, b, small_sem.at[i])
        for i, (a, b) in enumerate(
            [
                (occ_hbm, occ_ref), (off_hbm, off_ref), (tc_hbm, tc_ref),
                (idx_hbm, idx_ref), (orb_hbm, orb_ref),
            ]
        )
    ]
    for copy in small:
        copy.start()
    on_each_chip(lambda place: pl.semaphore_wait(barrier, 1 + len(partners(place))))

    def raw_copy(side):
        return pltpu.make_async_remote_copy(
            src_ref=g_ref.at[:, :, pl.ds((1 - core) * HALF, HALF)],
            dst_ref=raw.at[side],
            send_sem=raw_send,
            recv_sem=raw_recv,
            device_id=sibling,
            device_id_type=MESH,
        )

    raw_copy(core).start()
    own.wait()
    raw_copy(1 - core).wait_recv()

    for pair in range(3):
        for e in range(2):
            for side in range(2):
                for q in range(KB):
                    n = pair * ROWS + e * 8 + side * KB + q
                    spread_rows[pl.ds(n * RAWSTEP, HALF), :] = raw[
                        side, 2 * pair + e, q
                    ].astype(F32)

    def turn(r, carry):
        for pair in range(3):
            rows = spread_rows[
                pl.ds(pair * ROWS * RAWSTEP + r, ROWS, stride=RAWSTEP), :
            ]
            buf[pair + 1, chip, core * HALF + r] = rows.astype(BF16)
        return carry

    lax.fori_loop(0, HALF, turn, 0, unroll=8)

    def rows_of(slot, side, chunk):
        return buf.at[slot[0], slot[1], pl.ds(side * HALF + chunk * CHUNK, CHUNK)]

    def number(slot, chunk):
        return (slot[0] * CHIPS + slot[1]) * 2 + chunk

    def ici_copy(now, link, step, there, slot, to, chunk):
        return pltpu.make_async_remote_copy(
            src_ref=rows_of(slot, core, chunk),
            dst_ref=rows_of(to, core, chunk),
            send_sem=ici_send.at[LINKS.index(link), now % CAP],
            recv_sem=ici_recv.at[number(to, chunk)],
            device_id=device(step, there),
            device_id_type=MESH,
        )

    def sib_copy(slot, chunk, side):
        return pltpu.make_async_remote_copy(
            src_ref=rows_of(slot, side, chunk),
            dst_ref=rows_of(slot, side, chunk),
            send_sem=sib_send.at[number(slot, chunk)],
            recv_sem=sib_recv.at[number(slot, chunk)],
            device_id=sibling,
            device_id_type=MESH,
        )

    got = [set() for _ in range(CHIPS)]

    def receive(place, chunks):
        for slot, chunk in chunks:
            if (slot, chunk) not in got[place]:
                got[place].add((slot, chunk))
                ici_copy(0, "up", 0, 0, slot, slot, chunk).wait_recv()
                sib_copy(slot, chunk, core).start()

    def steps(first, last):
        def act(place):
            for now in range(first, last):
                if CAP <= now < STEPS + CAP:
                    for copy in outgoing[place][now - CAP]:
                        ici_copy(now - CAP, *copy).wait_send()
                if now < STEPS:
                    for copy in outgoing[place][now]:
                        slot, chunk = copy[3], copy[5]
                        if slot[1] != place or slot[0] in (0, 4):
                            receive(place, [(slot, chunk)])
                        ici_copy(now, *copy).start()
                if now == 0:
                    for pair in (1, 2, 3):
                        for chunk in range(2):
                            sib_copy((pair, place), chunk, core).start()
                if LAG <= now < STEPS + LAG:
                    receive(place, incoming[place][now - LAG])

        on_each_chip(act)

    waited = [set() for _ in range(CHIPS)]

    def from_sibling(which):
        def act(place):
            for t in which(place):
                for slot in [(t + p, s) for p in range(3) for s in range(CHIPS)]:
                    if slot not in waited[place]:
                        waited[place].add(slot)
                        for chunk in range(2):
                            sib_copy(slot, chunk, 1 - core).wait_recv()

        on_each_chip(act)

    steps(0, 2)
    for copy in small:
        copy.wait()

    column = lax.broadcasted_iota(jnp.int32, (NK, DEPTH), 1)
    source = lax.div(lax.rem(column, CHIPS * ROWS), ROWS) * 8 + lax.rem(column, 8)
    label = lax.broadcasted_iota(jnp.int32, (NK, DEPTH), 0)
    widen = (source == label).astype(F32).astype(BF16)
    target = lax.broadcasted_iota(jnp.int32, (8, NK), 0) + mom * KB
    pick = (target == lax.broadcasted_iota(jnp.int32, (8, NK), 1)).astype(F32).astype(BF16)
    table = idx_ref[...].astype(F32).astype(BF16)
    table = jnp.dot(pick, table, preferred_element_type=F32).astype(BF16)
    table = jnp.dot(table, widen, preferred_element_type=F32)
    mode = lax.broadcasted_iota(jnp.int32, (NW, DEPTH), 0)
    occ = jnp.zeros((NW, DEPTH), F32)
    off = jnp.zeros((NW, DEPTH), jnp.int32)
    for w in range(NW):
        occ = jnp.where(mode == w, occ_ref[w], occ)
        off = jnp.where(mode == w, off_ref[w], off)
    place_of = lax.broadcasted_iota(jnp.int32, (NW, DEPTH), 1)
    pair_of = lax.div(place_of, CHIPS * ROWS)
    energy_of = 2 * (pair_of - 1) + lax.div(lax.rem(place_of, ROWS), 8)
    first = (energy > 0).astype(F32)
    last = (energy < energies - 1).astype(F32)
    values = [[] for _ in range(2)]
    for k in range(KB):
        chosen = (table[k : k + 1, :] == label.astype(F32)).astype(F32).astype(BF16)
        spread = jnp.dot(tc_ref[...], chosen, preferred_element_type=F32)
        low = (occ * spread).astype(BF16).astype(F32)
        high = ((occ + 1.0) * spread).astype(BF16).astype(F32)
        for e in range(2):
            away = energy_of - e
            value = jnp.where(away < 0, low, high)
            values[e].append(jnp.where(jnp.abs(away) == off, value, 0.0))
    value = jnp.concatenate(values[0] + values[1], axis=0)
    pair_of = lax.div(lax.broadcasted_iota(jnp.int32, (TGT, DEPTH), 1), CHIPS * ROWS)
    for t, kept in ((0, first), (1, None), (2, last)):
        now = value if kept is None else jnp.where(pair_of == t, value * kept, value)
        weights[t] = now.astype(BF16)
        above = jnp.zeros((SHIFT, DEPTH), F32)
        below = jnp.zeros((ODD - TGT - SHIFT, DEPTH), F32)
        odd_weights[t] = jnp.concatenate([above, now, below], axis=0).astype(BF16)

    for w in range(NW):
        real = orb_ref[w, 0].astype(F32)
        imag = orb_ref[w, 1].astype(F32)
        top = jnp.concatenate([real, imag], axis=1)
        bottom = jnp.concatenate([-imag, real], axis=1)
        left_mats[w] = top.astype(BF16)
        right_mats[pl.ds(w * 128, 128), :] = jnp.concatenate([top, bottom], axis=0).T.astype(BF16)

    def mix(t, first, last):
        def one(i, carry):
            for odd, matrix in enumerate((weights, odd_weights)):
                wide = []
                for r in (4 * i + odd, 4 * i + odd + 2):
                    parts = [buf[t + p, s, r] for p in range(3) for s in range(CHIPS)]
                    wide.append(jnp.concatenate(parts, axis=0))
                got = jnp.dot(
                    matrix[t], jnp.concatenate(wide, axis=1), preferred_element_type=F32
                )
                start = pl.multiple_of(4 * i * MIXSTEP + odd * (MIXSTEP - SHIFT), 8)
                mixed[pl.ds(start, matrix.shape[1]), :] = got[:, :128]
                start = pl.multiple_of(start + 2 * MIXSTEP, 8)
                mixed[pl.ds(start, matrix.shape[1]), :] = got[:, 128:]
            return carry

        lax.fori_loop(first // 4, last // 4, one, 0, unroll=(last - first) // 4)

    def modes(t, first, last):
        def one(i, total):
            lefts = []
            for w in (2 * i, 2 * i + 1):
                rows = []
                for j in range(KB):
                    stacked = []
                    for n in (2 * j, 2 * j + 1):
                        m = mixed[pl.ds(n * NW + w, NO, stride=MIXSTEP), :].astype(BF16)
                        turned = jnp.concatenate([-m[:, NO:], m[:, :NO]], axis=1)
                        stacked.append(jnp.concatenate([m, turned], axis=0))
                    both = jnp.concatenate(stacked, axis=1)
                    got = jnp.dot(left_mats[w], both, preferred_element_type=F32)
                    rows += [got[:, :128], got[:, 128:]]
                lefts.append(jnp.concatenate(rows, axis=0).astype(BF16))
            right = right_mats[pl.ds(pl.multiple_of(i * 256, 256), 256), :]
            rows_out = pl.ds(pl.multiple_of(t * OUT, OUT), OUT)
            stage[rows_out, :] += jnp.dot(
                jnp.concatenate(lefts, axis=1), right, preferred_element_type=F32
            )
            return total

        if first == 0:
            stage[pl.ds(pl.multiple_of(t * OUT, OUT), OUT), :] = jnp.zeros((OUT, 128), F32)
        lax.fori_loop(first // 2, last // 2, one, 0, unroll=(last - first) // 2)

    def out_copy(which):
        rows = pl.ds(pl.multiple_of(tps(which) * OUT, OUT), OUT)
        return pltpu.make_async_copy(stage.at[rows], out_ref.at[rows], out_sem.at[which])

    def needs(which):
        def act(place):
            t = order[place][which]
            receive(place, [c for row in incoming[place] for c in row if t <= c[0][0] <= t + 2])

        on_each_chip(act)

    def tps(which):
        return by_chip([o[which] for o in order])

    steps(2, head)
    needs(0)
    steps(head, head + 1)
    from_sibling(lambda place: order[place][:1])
    mix(tps(0), 0, NO // 2)
    steps(head + 1, head + 2)
    mix(tps(0), NO // 2, NO)
    steps(head + 2, head + 3)
    modes(tps(0), 0, NW // 2)
    steps(head + 3, head + 4)
    modes(tps(0), NW // 2, NW)
    out_copy(0).start()
    steps(head + 4, max(STEPS, head + 4))
    needs(1)
    from_sibling(lambda place: order[place][1:2])
    mix(tps(1), 0, NO)
    needs(2)
    steps(max(STEPS, head + 4), STEPS + max(CAP, LAG))
    modes(tps(1), 0, NW)
    out_copy(1).start()
    from_sibling(lambda place: order[place][2:])
    mix(tps(2), 0, NO)
    modes(tps(2), 0, NW)
    out_copy(2).start()

    raw_copy(core).wait_send()
    for which in range(3):
        out_copy(which).wait()

    def finish(place):
        for slot in [(p, s) for p in range(PAIRS) for s in range(CHIPS)]:
            for chunk in range(2):
                sib_copy(slot, chunk, core).wait_send()

    finish(0)


def body(green, occupation, coupling, orbital, offsets, index):
    hbm = pl.BlockSpec(memory_space=pltpu.HBM)
    slots = PAIRS * CHIPS * 2
    result = pl.pallas_call(
        kernel,
        out_shape=jax.ShapeDtypeStruct((3 * OUT, 128), F32),
        in_specs=[hbm] * 6,
        out_specs=hbm,
        scratch_shapes=[
            pltpu.VMEM((2, EB, KB, HALF, 128), BF16),
            pltpu.VMEM((3 * ROWS * RAWSTEP, 128), F32),
            pltpu.VMEM((PAIRS, CHIPS, NO, ROWS, 128), BF16),
            pltpu.VMEM((3, TGT, DEPTH), BF16),
            pltpu.VMEM((3, ODD, DEPTH), BF16),
            pltpu.VMEM((NW, NO, 128), BF16),
            pltpu.VMEM((NW * 128, 128), BF16),
            pltpu.VMEM((NO * MIXSTEP, 128), F32),
            pltpu.VMEM((3 * OUT, 128), F32),
            pltpu.SMEM((NW,), F32),
            pltpu.SMEM((NW,), jnp.int32),
            pltpu.VMEM((NW, NK), BF16),
            pltpu.VMEM((NK, NK), jnp.int32),
            pltpu.VMEM((NW, 2, NO, NO), BF16),
            pltpu.SemaphoreType.DMA((5,)),
            pltpu.SemaphoreType.DMA,
            pltpu.SemaphoreType.DMA,
            pltpu.SemaphoreType.DMA,
            pltpu.SemaphoreType.DMA((2, CAP)),
            pltpu.SemaphoreType.DMA((slots,)),
            pltpu.SemaphoreType.DMA((slots,)),
            pltpu.SemaphoreType.DMA((slots,)),
            pltpu.SemaphoreType.DMA((3,)),
        ],
        compiler_params=pltpu.CompilerParams(
            collective_id=0, has_side_effects=True, vmem_limit_bytes=56 * 1024 * 1024
        ),
    )(green, occupation, offsets, coupling, index, orbital)
    return result.reshape(green.shape)


def solution(mesh):
    placed = (P("energy", "mom", None, None), P(), P(), P(), P(), P())
    return jax.shard_map(
        body, mesh=mesh, in_specs=placed, out_specs=P("energy", "mom", None, None), check_vma=False
    )
```

```python
import jax
import jax.numpy as jnp
from jax import lax
from jax.experimental import pallas as pl
from jax.experimental.pallas import tpu as pltpu
from jax.sharding import PartitionSpec as P

MESH = pl.DeviceIdType.MESH
BF16 = jnp.bfloat16
F32 = jnp.float32

NO = 64
NW = 16
NK = 32
EB = 6
KB = 4
CHIPS = 4
PAIRS = 5
HALF = NO // 2
CHUNK = HALF // 2
ROWS = 16
DEPTH = 3 * CHIPS * ROWS
TGT = 2 * KB * NW
OUT = 2 * KB * NO
RAWSTEP = 36
SHIFT = 4
ODD = TGT + 16
MIXSTEP = TGT + 8 + SHIFT
LINKS = ("up", "down")

UP = (
    (
        (1, 0, 0), (1, 0, 1), (3, 0, 0), (3, 0, 1), (4, 3, 0), (4, 3, 1), (2, 0, 0), (2, 0, 1),
        (4, 2, 0), (4, 2, 1), (0, 3, 0), (0, 3, 1), (4, 1, 0), (4, 1, 1), (0, 1, 0), (0, 1, 1),
        (0, 2, 0), (0, 2, 1),
    ),
    (
        (1, 1, 0), (1, 1, 1), (3, 1, 0), (3, 1, 1), (1, 0, 0), (1, 0, 1), (3, 0, 0), (3, 0, 1),
        (4, 3, 0), (4, 3, 1), (2, 0, 0), (2, 0, 1), (2, 1, 0), (2, 1, 1), (0, 3, 0), (0, 3, 1),
    ),
    (
        (1, 2, 0), (1, 2, 1), (3, 2, 0), (3, 2, 1), (1, 1, 0), (1, 1, 1), (3, 1, 0), (3, 1, 1),
        (1, 0, 0), (1, 0, 1), (3, 0, 0), (3, 0, 1), (2, 2, 0), (2, 2, 1), (2, 0, 0), (2, 0, 1),
        (2, 1, 0), (2, 1, 1),
    ),
    (
        (1, 3, 0), (1, 3, 1), (3, 3, 0), (3, 3, 1), (1, 2, 0), (1, 2, 1), (3, 2, 0), (3, 2, 1),
        (1, 1, 0), (1, 1, 1), (3, 1, 0), (3, 1, 1), (1, 0, 0), (1, 0, 1), (3, 0, 0), (3, 0, 1),
    ),
)
CAP = 4
EARLY = 4
LAG = 3
STEPS = max(len(row) for row in UP)


def up_target(chip, slot):
    pair, source = slot
    if chip < CHIPS - 1:
        return 0, chip + 1, slot
    return (1, 0, (0, source)) if pair == 3 else (-1, 0, (4, source))


def plan():
    out = [[[] for _ in range(STEPS)] for _ in range(CHIPS)]
    into = [[[] for _ in range(STEPS)] for _ in range(CHIPS)]
    for chip in range(CHIPS):
        for now, entry in enumerate(UP[chip]):
            if not entry:
                continue
            slot, chunk = entry[:2], entry[2]
            step, there, to = up_target(chip, slot)
            out[chip][now].append(("up", step, there, slot, to, chunk))
            into[there][now].append((to, chunk))
            far = [(PAIRS - 1 - s[0], CHIPS - 1 - s[1]) for s in (slot, to)]
            here, there = CHIPS - 1 - chip, CHIPS - 1 - there
            out[here][now].append(("down", -step, there, far[0], far[1], chunk))
            into[there][now].append((far[1], chunk))
    return out, into


def kernel(
    g_ref, occ_hbm, off_hbm, tc_hbm, idx_hbm, orb_hbm, out_ref,
    raw, spread_rows, buf, weights, odd_weights, left_mats, right_mats, mixed, stage,
    occ_ref, off_ref, tc_ref, idx_ref, orb_ref,
    small_sem, own_sem, raw_send, raw_recv, ici_send, ici_recv, sib_send, sib_recv, out_sem,
):
    energies = lax.axis_size("energy")
    energy = lax.axis_index("energy")
    mom = lax.axis_index("mom")
    core = lax.rem(mom, 2)
    chip = lax.div(mom, 2)
    sibling = (energy, mom + 1 - 2 * core)
    outgoing, incoming = plan()
    late = max(now for rows in incoming for now, row in enumerate(rows) for _, c in row if c == 0)
    def device(step, there):
        return (lax.rem(energy + step + energies, energies), 2 * there + core)

    def partners(place):
        if place == 0:
            return [(1, CHIPS - 1), (-1, CHIPS - 1), (0, 1)]
        if place == CHIPS - 1:
            return [(1, 0), (-1, 0), (0, CHIPS - 2)]
        return [(0, place - 1), (0, place + 1)]

    def on_each_chip(act):
        for place in range(CHIPS):

            @pl.when(chip == place)
            def _(place=place):
                act(place)

    own = pltpu.make_async_copy(
        g_ref.at[:, :, pl.ds(core * HALF, HALF)], raw.at[core], own_sem
    )
    own.start()
    barrier = pltpu.get_barrier_semaphore()
    pl.semaphore_signal(barrier, inc=1, device_id=sibling, device_id_type=MESH)

    def greet(place):
        for step, there in partners(place):
            pl.semaphore_signal(
                barrier, inc=1, device_id=device(step, there), device_id_type=MESH
            )

    on_each_chip(greet)
    small = [
        pltpu.make_async_copy(a, b, small_sem.at[i])
        for i, (a, b) in enumerate(
            [
                (occ_hbm, occ_ref), (off_hbm, off_ref), (tc_hbm, tc_ref),
                (idx_hbm, idx_ref), (orb_hbm, orb_ref),
            ]
        )
    ]
    for copy in small:
        copy.start()
    on_each_chip(lambda place: pl.semaphore_wait(barrier, 1 + len(partners(place))))

    def raw_copy(side):
        return pltpu.make_async_remote_copy(
            src_ref=g_ref.at[:, :, pl.ds((1 - core) * HALF, HALF)],
            dst_ref=raw.at[side],
            send_sem=raw_send,
            recv_sem=raw_recv,
            device_id=sibling,
            device_id_type=MESH,
        )

    raw_copy(core).start()
    own.wait()
    raw_copy(1 - core).wait_recv()

    def turn(pairs):
        for pair in pairs:
            for e in range(2):
                for side in range(2):
                    for q in range(KB):
                        n = pair * ROWS + e * 8 + side * KB + q
                        spread_rows[pl.ds(n * RAWSTEP, HALF), :] = raw[
                            side, 2 * pair + e, q
                        ].astype(F32)

        def one(r, carry):
            for pair in pairs:
                rows = spread_rows[
                    pl.ds(pair * ROWS * RAWSTEP + r, ROWS, stride=RAWSTEP), :
                ]
                buf[pair + 1, chip, core * HALF + r] = rows.astype(BF16)
            return carry

        lax.fori_loop(0, HALF, one, 0, unroll=16)

    def rows_of(slot, side, chunk):
        return buf.at[slot[0], slot[1], pl.ds(side * HALF + chunk * CHUNK, CHUNK)]

    def number(slot, chunk):
        return (slot[0] * CHIPS + slot[1]) * 2 + chunk

    def ici_copy(now, link, step, there, slot, to, chunk):
        return pltpu.make_async_remote_copy(
            src_ref=rows_of(slot, core, chunk),
            dst_ref=rows_of(to, core, chunk),
            send_sem=ici_send.at[LINKS.index(link), now % CAP],
            recv_sem=ici_recv.at[number(to, chunk)],
            device_id=device(step, there),
            device_id_type=MESH,
        )

    def sib_copy(slot, chunk, side):
        return pltpu.make_async_remote_copy(
            src_ref=rows_of(slot, side, chunk),
            dst_ref=rows_of(slot, side, chunk),
            send_sem=sib_send.at[number(slot, chunk)],
            recv_sem=sib_recv.at[number(slot, chunk)],
            device_id=sibling,
            device_id_type=MESH,
        )

    got = [set() for _ in range(CHIPS)]

    def receive(place, chunks):
        for slot, chunk in chunks:
            if (slot, chunk) not in got[place]:
                got[place].add((slot, chunk))
                ici_copy(0, "up", 0, 0, slot, slot, chunk).wait_recv()
                sib_copy(slot, chunk, core).start()

    def steps(first, last):
        def act(place):
            for now in range(first, last):
                if CAP <= now < STEPS + CAP:
                    for copy in outgoing[place][now - CAP]:
                        ici_copy(now - CAP, *copy).wait_send()
                if now < STEPS:
                    for copy in outgoing[place][now]:
                        slot, chunk = copy[3], copy[5]
                        if slot[1] != place or slot[0] in (0, 4):
                            receive(place, [(slot, chunk)])
                        ici_copy(now, *copy).start()
                if LAG <= now < STEPS + LAG:
                    receive(place, incoming[place][now - LAG])

        on_each_chip(act)

    def from_sibling(chunk):
        for pair in range(PAIRS):
            for source in range(CHIPS):
                sib_copy((pair, source), chunk, 1 - core).wait_recv()

    early = [row[:EARLY] for row in UP]
    assert all(not c or c[1] == i and c[0] != 2 for i, row in enumerate(early) for c in row)
    turn((0, 2))
    steps(0, EARLY)
    turn((1,))

    def own_to_sibling(place):
        for pair in (1, 2, 3):
            for chunk in range(2):
                sib_copy((pair, place), chunk, core).start()

    on_each_chip(own_to_sibling)
    for copy in small:
        copy.wait()

    column = lax.broadcasted_iota(jnp.int32, (NK, DEPTH), 1)
    source = lax.div(lax.rem(column, CHIPS * ROWS), ROWS) * 8 + lax.rem(column, 8)
    label = lax.broadcasted_iota(jnp.int32, (NK, DEPTH), 0)
    widen = (source == label).astype(F32).astype(BF16)
    target = lax.broadcasted_iota(jnp.int32, (8, NK), 0) + mom * KB
    pick = (target == lax.broadcasted_iota(jnp.int32, (8, NK), 1)).astype(F32).astype(BF16)
    table = idx_ref[...].astype(F32).astype(BF16)
    table = jnp.dot(pick, table, preferred_element_type=F32).astype(BF16)
    table = jnp.dot(table, widen, preferred_element_type=F32)
    mode = lax.broadcasted_iota(jnp.int32, (NW, DEPTH), 0)
    occ = jnp.zeros((NW, DEPTH), F32)
    off = jnp.zeros((NW, DEPTH), jnp.int32)
    for w in range(NW):
        occ = jnp.where(mode == w, occ_ref[w], occ)
        off = jnp.where(mode == w, off_ref[w], off)
    place_of = lax.broadcasted_iota(jnp.int32, (NW, DEPTH), 1)
    pair_of = lax.div(place_of, CHIPS * ROWS)
    energy_of = 2 * (pair_of - 1) + lax.div(lax.rem(place_of, ROWS), 8)
    first = (energy > 0).astype(F32)
    last = (energy < energies - 1).astype(F32)
    values = [[] for _ in range(2)]
    for k in range(KB):
        chosen = (table[k : k + 1, :] == label.astype(F32)).astype(F32).astype(BF16)
        spread = jnp.dot(tc_ref[...], chosen, preferred_element_type=F32)
        low = (occ * spread).astype(BF16).astype(F32)
        high = ((occ + 1.0) * spread).astype(BF16).astype(F32)
        for e in range(2):
            away = energy_of - e
            value = jnp.where(away < 0, low, high)
            values[e].append(jnp.where(jnp.abs(away) == off, value, 0.0))
    value = jnp.concatenate(values[0] + values[1], axis=0)
    pair_of = lax.div(lax.broadcasted_iota(jnp.int32, (TGT, DEPTH), 1), CHIPS * ROWS)
    for t, kept in ((0, first), (1, None), (2, last)):
        now = value if kept is None else jnp.where(pair_of == t, value * kept, value)
        weights[t] = now.astype(BF16)
        above = jnp.zeros((SHIFT, DEPTH), F32)
        below = jnp.zeros((ODD - TGT - SHIFT, DEPTH), F32)
        odd_weights[t] = jnp.concatenate([above, now, below], axis=0).astype(BF16)

    for w in range(NW):
        real = orb_ref[w, 0].astype(F32)
        imag = orb_ref[w, 1].astype(F32)
        top = jnp.concatenate([real, imag], axis=1)
        bottom = jnp.concatenate([-imag, real], axis=1)
        left_mats[w] = top.astype(BF16)
        right_mats[pl.ds(w * 128, 128), :] = jnp.concatenate([top, bottom], axis=0).T.astype(BF16)

    def mix(side, chunk):
        base = side * HALF + chunk * CHUNK

        def one(t, carry):
            for i in range(CHUNK // 4):
                for odd, matrix in enumerate((weights, odd_weights)):
                    wide = []
                    for r in (4 * i + odd, 4 * i + odd + 2):
                        parts = [buf[t + p, s, base + r] for p in range(3) for s in range(CHIPS)]
                        wide.append(jnp.concatenate(parts, axis=0))
                    got = jnp.dot(
                        matrix[t], jnp.concatenate(wide, axis=1), preferred_element_type=F32
                    )
                    start = (t * NO + base + 4 * i) * MIXSTEP + odd * (MIXSTEP - SHIFT)
                    mixed[pl.ds(pl.multiple_of(start, 8), matrix.shape[1]), :] = got[:, :128]
                    start = start + 2 * MIXSTEP
                    mixed[pl.ds(pl.multiple_of(start, 8), matrix.shape[1]), :] = got[:, 128:]
            return carry

        lax.fori_loop(0, 3, one, 0)

    def out_copy(t):
        rows = pl.ds(pl.multiple_of(t * OUT, OUT), OUT)
        return pltpu.make_async_copy(stage.at[rows], out_ref.at[rows], out_sem.at[t])

    def modes(t, carry):
        rows_out = pl.ds(pl.multiple_of(t * OUT, OUT), OUT)
        for i in range(NW // 2):
            lefts = []
            for w in (2 * i, 2 * i + 1):
                rows = []
                for j in range(KB):
                    stacked = []
                    for n in (2 * j, 2 * j + 1):
                        start = t * (NO * MIXSTEP) + n * NW + w
                        m = mixed[pl.ds(start, NO, stride=MIXSTEP), :].astype(BF16)
                        turned = jnp.concatenate([-m[:, NO:], m[:, :NO]], axis=1)
                        stacked.append(jnp.concatenate([m, turned], axis=0))
                    both = jnp.concatenate(stacked, axis=1)
                    got = jnp.dot(left_mats[w], both, preferred_element_type=F32)
                    rows += [got[:, :128], got[:, 128:]]
                lefts.append(jnp.concatenate(rows, axis=0).astype(BF16))
            right = right_mats[pl.ds(i * 256, 256), :]
            part = jnp.dot(jnp.concatenate(lefts, axis=1), right, preferred_element_type=F32)
            if i == 0:
                stage[rows_out, :] = part
            else:
                stage[rows_out, :] += part
        out_copy(t).start()
        return carry

    steps(EARLY, late + LAG + 1)
    mix(core, 0)
    from_sibling(0)
    mix(1 - core, 0)
    steps(late + LAG + 1, STEPS + max(CAP, LAG))
    mix(core, 1)
    from_sibling(1)
    mix(1 - core, 1)
    lax.fori_loop(0, 3, modes, 0)

    raw_copy(core).wait_send()
    for t in range(3):
        out_copy(t).wait()

    def finish(place):
        for slot in [(p, s) for p in range(PAIRS) for s in range(CHIPS)]:
            for chunk in range(2):
                sib_copy(slot, chunk, core).wait_send()

    finish(0)


def body(green, occupation, coupling, orbital, offsets, index):
    hbm = pl.BlockSpec(memory_space=pltpu.HBM)
    slots = PAIRS * CHIPS * 2
    result = pl.pallas_call(
        kernel,
        out_shape=jax.ShapeDtypeStruct((3 * OUT, 128), F32),
        in_specs=[hbm] * 6,
        out_specs=hbm,
        scratch_shapes=[
            pltpu.VMEM((2, EB, KB, HALF, 128), BF16),
            pltpu.VMEM((3 * ROWS * RAWSTEP, 128), F32),
            pltpu.VMEM((PAIRS, CHIPS, NO, ROWS, 128), BF16),
            pltpu.VMEM((3, TGT, DEPTH), BF16),
            pltpu.VMEM((3, ODD, DEPTH), BF16),
            pltpu.VMEM((NW, NO, 128), BF16),
            pltpu.VMEM((NW * 128, 128), BF16),
            pltpu.VMEM((3 * NO * MIXSTEP, 128), F32),
            pltpu.VMEM((3 * OUT, 128), F32),
            pltpu.SMEM((NW,), F32),
            pltpu.SMEM((NW,), jnp.int32),
            pltpu.VMEM((NW, NK), BF16),
            pltpu.VMEM((NK, NK), jnp.int32),
            pltpu.VMEM((NW, 2, NO, NO), BF16),
            pltpu.SemaphoreType.DMA((5,)),
            pltpu.SemaphoreType.DMA,
            pltpu.SemaphoreType.DMA,
            pltpu.SemaphoreType.DMA,
            pltpu.SemaphoreType.DMA((2, CAP)),
            pltpu.SemaphoreType.DMA((slots,)),
            pltpu.SemaphoreType.DMA((slots,)),
            pltpu.SemaphoreType.DMA((slots,)),
            pltpu.SemaphoreType.DMA((3,)),
        ],
        compiler_params=pltpu.CompilerParams(
            collective_id=0, has_side_effects=True, vmem_limit_bytes=56 * 1024 * 1024
        ),
    )(green, occupation, offsets, coupling, index, orbital)
    return result.reshape(green.shape)


def solution(mesh):
    placed = (P("energy", "mom", None, None), P(), P(), P(), P(), P())
    return jax.shard_map(
        body, mesh=mesh, in_specs=placed, out_specs=P("energy", "mom", None, None), check_vma=False
    )
```

```python
import jax
import jax.numpy as jnp
from jax import lax
from jax.experimental import pallas as pl
from jax.experimental.pallas import tpu as pltpu
from jax.sharding import PartitionSpec as P

MESH = pl.DeviceIdType.MESH
BF16 = jnp.bfloat16
F32 = jnp.float32

NO = 64
NW = 16
NK = 32
EB = 6
KB = 4
CHIPS = 4
PAIRS = 5
HALF = NO // 2
CHUNK = HALF // 2
ROWS = 16
DEPTH = 3 * CHIPS * ROWS
TGT = 2 * KB * NW
OUT = 2 * KB * NO
RAWSTEP = 36
SHIFT = 4
ODD = TGT + 16
MIXSTEP = TGT + 8 + SHIFT
LINKS = ("up", "down")

UP = (
    (
        (1, 0, 0), (1, 0, 1), (3, 0, 0), (3, 0, 1), (4, 3, 0), (4, 3, 1), (2, 0, 0), (2, 0, 1),
        (4, 2, 0), (4, 2, 1), (0, 3, 0), (0, 3, 1), (4, 1, 0), (4, 1, 1), (0, 1, 0), (0, 1, 1),
        (0, 2, 0), (0, 2, 1),
    ),
    (
        (1, 1, 0), (1, 1, 1), (3, 1, 0), (3, 1, 1), (1, 0, 0), (1, 0, 1), (3, 0, 0), (3, 0, 1),
        (4, 3, 0), (4, 3, 1), (2, 0, 0), (2, 0, 1), (2, 1, 0), (2, 1, 1), (0, 3, 0), (0, 3, 1),
    ),
    (
        (1, 2, 0), (1, 2, 1), (3, 2, 0), (3, 2, 1), (1, 1, 0), (1, 1, 1), (3, 1, 0), (3, 1, 1),
        (1, 0, 0), (1, 0, 1), (3, 0, 0), (3, 0, 1), (2, 2, 0), (2, 2, 1), (2, 0, 0), (2, 0, 1),
        (2, 1, 0), (2, 1, 1),
    ),
    (
        (1, 3, 0), (1, 3, 1), (3, 3, 0), (3, 3, 1), (1, 2, 0), (1, 2, 1), (3, 2, 0), (3, 2, 1),
        (1, 1, 0), (1, 1, 1), (3, 1, 0), (3, 1, 1), (1, 0, 0), (1, 0, 1), (3, 0, 0), (3, 0, 1),
    ),
)
CAP = 4
EARLY = 4
LAG = 3
STEPS = max(len(row) for row in UP)


def up_target(chip, slot):
    pair, source = slot
    if chip < CHIPS - 1:
        return 0, chip + 1, slot
    return (1, 0, (0, source)) if pair == 3 else (-1, 0, (4, source))


def plan():
    out = [[[] for _ in range(STEPS)] for _ in range(CHIPS)]
    into = [[[] for _ in range(STEPS)] for _ in range(CHIPS)]
    for chip in range(CHIPS):
        for now, entry in enumerate(UP[chip]):
            if not entry:
                continue
            slot, chunk = entry[:2], entry[2]
            step, there, to = up_target(chip, slot)
            out[chip][now].append(("up", step, there, slot, to, chunk))
            into[there][now].append((to, chunk))
            far = [(PAIRS - 1 - s[0], CHIPS - 1 - s[1]) for s in (slot, to)]
            here, there = CHIPS - 1 - chip, CHIPS - 1 - there
            out[here][now].append(("down", -step, there, far[0], far[1], chunk))
            into[there][now].append((far[1], chunk))
    return out, into


def kernel(
    g_ref, occ_hbm, off_hbm, tc_hbm, idx_hbm, orb_hbm, out_ref,
    raw, spread_rows, buf, weights, odd_weights, left_mats, right_mats, mixed,
    occ_ref, off_ref, tc_ref, idx_ref, orb_ref,
    small_sem, own_sem, raw_send, raw_recv, ici_send, ici_recv, sib_send, sib_recv,
):
    energies = lax.axis_size("energy")
    energy = lax.axis_index("energy")
    mom = lax.axis_index("mom")
    core = lax.rem(mom, 2)
    chip = lax.div(mom, 2)
    sibling = (energy, mom + 1 - 2 * core)
    outgoing, incoming = plan()
    late = max(now for rows in incoming for now, row in enumerate(rows) for _, c in row if c == 0)
    def device(step, there):
        return (lax.rem(energy + step + energies, energies), 2 * there + core)

    def partners(place):
        if place == 0:
            return [(1, CHIPS - 1), (-1, CHIPS - 1), (0, 1)]
        if place == CHIPS - 1:
            return [(1, 0), (-1, 0), (0, CHIPS - 2)]
        return [(0, place - 1), (0, place + 1)]

    def on_each_chip(act):
        for place in range(CHIPS):

            @pl.when(chip == place)
            def _(place=place):
                act(place)

    own = pltpu.make_async_copy(
        g_ref.at[:, :, pl.ds(core * HALF, HALF)], raw.at[core], own_sem
    )
    own.start()
    barrier = pltpu.get_barrier_semaphore()
    pl.semaphore_signal(barrier, inc=1, device_id=sibling, device_id_type=MESH)

    def greet(place):
        for step, there in partners(place):
            pl.semaphore_signal(
                barrier, inc=1, device_id=device(step, there), device_id_type=MESH
            )

    on_each_chip(greet)
    small = [
        pltpu.make_async_copy(a, b, small_sem.at[i])
        for i, (a, b) in enumerate(
            [
                (occ_hbm, occ_ref), (off_hbm, off_ref), (tc_hbm, tc_ref),
                (idx_hbm, idx_ref), (orb_hbm, orb_ref),
            ]
        )
    ]
    for copy in small:
        copy.start()
    on_each_chip(lambda place: pl.semaphore_wait(barrier, 1 + len(partners(place))))

    def raw_copy(side):
        return pltpu.make_async_remote_copy(
            src_ref=g_ref.at[:, :, pl.ds((1 - core) * HALF, HALF)],
            dst_ref=raw.at[side],
            send_sem=raw_send,
            recv_sem=raw_recv,
            device_id=sibling,
            device_id_type=MESH,
        )

    raw_copy(core).start()
    own.wait()
    raw_copy(1 - core).wait_recv()

    def turn(pairs):
        for pair in pairs:
            for e in range(2):
                for side in range(2):
                    for q in range(KB):
                        n = pair * ROWS + e * 8 + side * KB + q
                        spread_rows[pl.ds(n * RAWSTEP, HALF), :] = raw[
                            side, 2 * pair + e, q
                        ].astype(F32)

        def one(r, carry):
            for pair in pairs:
                rows = spread_rows[
                    pl.ds(pair * ROWS * RAWSTEP + r, ROWS, stride=RAWSTEP), :
                ]
                buf[pair + 1, chip, core * HALF + r] = rows.astype(BF16)
            return carry

        lax.fori_loop(0, HALF, one, 0, unroll=16)

    def rows_of(slot, side, chunk):
        return buf.at[slot[0], slot[1], pl.ds(side * HALF + chunk * CHUNK, CHUNK)]

    def number(slot, chunk):
        return (slot[0] * CHIPS + slot[1]) * 2 + chunk

    def ici_copy(now, link, step, there, slot, to, chunk):
        return pltpu.make_async_remote_copy(
            src_ref=rows_of(slot, core, chunk),
            dst_ref=rows_of(to, core, chunk),
            send_sem=ici_send.at[LINKS.index(link), now % CAP],
            recv_sem=ici_recv.at[number(to, chunk)],
            device_id=device(step, there),
            device_id_type=MESH,
        )

    def sib_copy(slot, chunk, side):
        return pltpu.make_async_remote_copy(
            src_ref=rows_of(slot, side, chunk),
            dst_ref=rows_of(slot, side, chunk),
            send_sem=sib_send.at[number(slot, chunk)],
            recv_sem=sib_recv.at[number(slot, chunk)],
            device_id=sibling,
            device_id_type=MESH,
        )

    got = [set() for _ in range(CHIPS)]

    def receive(place, chunks):
        for slot, chunk in chunks:
            if (slot, chunk) not in got[place]:
                got[place].add((slot, chunk))
                ici_copy(0, "up", 0, 0, slot, slot, chunk).wait_recv()
                sib_copy(slot, chunk, core).start()

    def steps(first, last):
        def act(place):
            for now in range(first, last):
                if CAP <= now < STEPS + CAP:
                    for copy in outgoing[place][now - CAP]:
                        ici_copy(now - CAP, *copy).wait_send()
                if now < STEPS:
                    for copy in outgoing[place][now]:
                        slot, chunk = copy[3], copy[5]
                        if slot[1] != place or slot[0] in (0, 4):
                            receive(place, [(slot, chunk)])
                        ici_copy(now, *copy).start()
                if LAG <= now < STEPS + LAG:
                    receive(place, incoming[place][now - LAG])

        on_each_chip(act)

    def from_sibling(chunk):
        for pair in range(PAIRS):
            for source in range(CHIPS):
                sib_copy((pair, source), chunk, 1 - core).wait_recv()

    outer_first = all(not c or c[0] != 2 for row in UP for c in row[:EARLY])
    turn((0, 2) if outer_first else (0, 1, 2))
    steps(0, EARLY)
    if outer_first:
        turn((1,))

    def own_to_sibling(place):
        for pair in (1, 2, 3):
            for chunk in range(2):
                sib_copy((pair, place), chunk, core).start()

    on_each_chip(own_to_sibling)
    for copy in small:
        copy.wait()

    column = lax.broadcasted_iota(jnp.int32, (NK, DEPTH), 1)
    source = lax.div(lax.rem(column, CHIPS * ROWS), ROWS) * 8 + lax.rem(column, 8)
    label = lax.broadcasted_iota(jnp.int32, (NK, DEPTH), 0)
    widen = (source == label).astype(F32).astype(BF16)
    target = lax.broadcasted_iota(jnp.int32, (8, NK), 0) + mom * KB
    pick = (target == lax.broadcasted_iota(jnp.int32, (8, NK), 1)).astype(F32).astype(BF16)
    table = idx_ref[...].astype(F32).astype(BF16)
    table = jnp.dot(pick, table, preferred_element_type=F32).astype(BF16)
    table = jnp.dot(table, widen, preferred_element_type=F32)
    mode = lax.broadcasted_iota(jnp.int32, (NW, DEPTH), 0)
    occ = jnp.zeros((NW, DEPTH), F32)
    off = jnp.zeros((NW, DEPTH), jnp.int32)
    for w in range(NW):
        occ = jnp.where(mode == w, occ_ref[w], occ)
        off = jnp.where(mode == w, off_ref[w], off)
    place_of = lax.broadcasted_iota(jnp.int32, (NW, DEPTH), 1)
    pair_of = lax.div(place_of, CHIPS * ROWS)
    energy_of = 2 * (pair_of - 1) + lax.div(lax.rem(place_of, ROWS), 8)
    first = (energy > 0).astype(F32)
    last = (energy < energies - 1).astype(F32)
    values = [[] for _ in range(2)]
    for k in range(KB):
        chosen = (table[k : k + 1, :] == label.astype(F32)).astype(F32).astype(BF16)
        spread = jnp.dot(tc_ref[...], chosen, preferred_element_type=F32)
        low = (occ * spread).astype(BF16).astype(F32)
        high = ((occ + 1.0) * spread).astype(BF16).astype(F32)
        for e in range(2):
            away = energy_of - e
            value = jnp.where(away < 0, low, high)
            values[e].append(jnp.where(jnp.abs(away) == off, value, 0.0))
    value = jnp.concatenate(values[0] + values[1], axis=0)
    pair_of = lax.div(lax.broadcasted_iota(jnp.int32, (TGT, DEPTH), 1), CHIPS * ROWS)
    for t, kept in ((0, first), (1, None), (2, last)):
        now = value if kept is None else jnp.where(pair_of == t, value * kept, value)
        weights[t] = now.astype(BF16)
        above = jnp.zeros((SHIFT, DEPTH), F32)
        below = jnp.zeros((ODD - TGT - SHIFT, DEPTH), F32)
        odd_weights[t] = jnp.concatenate([above, now, below], axis=0).astype(BF16)

    for w in range(NW):
        real = orb_ref[w, 0].astype(F32)
        imag = orb_ref[w, 1].astype(F32)
        top = jnp.concatenate([real, imag], axis=1)
        bottom = jnp.concatenate([-imag, real], axis=1)
        left_mats[w] = top.astype(BF16)
        right_mats[pl.ds(w * 128, 128), :] = jnp.concatenate([top, bottom], axis=0).T.astype(BF16)

    def mix(side, chunk):
        base = side * HALF + chunk * CHUNK

        def one(t, carry):
            for i in range(CHUNK // 4):
                for odd, matrix in enumerate((weights, odd_weights)):
                    wide = []
                    for r in (4 * i + odd, 4 * i + odd + 2):
                        parts = [buf[t + p, s, base + r] for p in range(3) for s in range(CHIPS)]
                        wide.append(jnp.concatenate(parts, axis=0))
                    got = jnp.dot(
                        matrix[t], jnp.concatenate(wide, axis=1), preferred_element_type=F32
                    )
                    start = (t * NO + base + 4 * i) * MIXSTEP + odd * (MIXSTEP - SHIFT)
                    mixed[pl.ds(pl.multiple_of(start, 8), matrix.shape[1]), :] = got[:, :128]
                    start = start + 2 * MIXSTEP
                    mixed[pl.ds(pl.multiple_of(start, 8), matrix.shape[1]), :] = got[:, 128:]
            return carry

        lax.fori_loop(0, 3, one, 0)

    def modes(t, carry):
        rows_out = pl.ds(pl.multiple_of(t * OUT, OUT), OUT)
        for i in range(NW // 2):
            lefts = []
            for w in (2 * i, 2 * i + 1):
                rows = []
                for j in range(KB):
                    stacked = []
                    for n in (2 * j, 2 * j + 1):
                        start = t * (NO * MIXSTEP) + n * NW + w
                        m = mixed[pl.ds(start, NO, stride=MIXSTEP), :].astype(BF16)
                        turned = jnp.concatenate([-m[:, NO:], m[:, :NO]], axis=1)
                        stacked.append(jnp.concatenate([m, turned], axis=0))
                    both = jnp.concatenate(stacked, axis=1)
                    got = jnp.dot(left_mats[w], both, preferred_element_type=F32)
                    rows += [got[:, :128], got[:, 128:]]
                lefts.append(jnp.concatenate(rows, axis=0).astype(BF16))
            right = right_mats[pl.ds(i * 256, 256), :]
            part = jnp.dot(jnp.concatenate(lefts, axis=1), right, preferred_element_type=F32)
            if i == 0:
                out_ref[rows_out, :] = part
            else:
                out_ref[rows_out, :] += part
        return carry

    steps(EARLY, late + LAG + 1)
    mix(core, 0)
    from_sibling(0)
    mix(1 - core, 0)
    steps(late + LAG + 1, STEPS + max(CAP, LAG))
    mix(core, 1)
    from_sibling(1)
    mix(1 - core, 1)
    lax.fori_loop(0, 3, modes, 0)

    raw_copy(core).wait_send()

    def finish(place):
        for slot in [(p, s) for p in range(PAIRS) for s in range(CHIPS)]:
            for chunk in range(2):
                sib_copy(slot, chunk, core).wait_send()

    finish(0)


def body(green, occupation, coupling, orbital, offsets, index):
    hbm = pl.BlockSpec(memory_space=pltpu.HBM)
    operands = [
        pltpu.with_memory_space_constraint(a, pltpu.HBM)
        for a in (green, occupation, offsets, coupling, index, orbital)
    ]
    slots = PAIRS * CHIPS * 2
    result = pl.pallas_call(
        kernel,
        out_shape=jax.ShapeDtypeStruct((3 * OUT, 128), F32),
        in_specs=[hbm] * 6,
        out_specs=pl.BlockSpec(memory_space=pltpu.VMEM),
        scratch_shapes=[
            pltpu.VMEM((2, EB, KB, HALF, 128), BF16),
            pltpu.VMEM((3 * ROWS * RAWSTEP, 128), F32),
            pltpu.VMEM((PAIRS, CHIPS, NO, ROWS, 128), BF16),
            pltpu.VMEM((3, TGT, DEPTH), BF16),
            pltpu.VMEM((3, ODD, DEPTH), BF16),
            pltpu.VMEM((NW, NO, 128), BF16),
            pltpu.VMEM((NW * 128, 128), BF16),
            pltpu.VMEM((3 * NO * MIXSTEP, 128), F32),
            pltpu.SMEM((NW,), F32),
            pltpu.SMEM((NW,), jnp.int32),
            pltpu.VMEM((NW, NK), BF16),
            pltpu.VMEM((NK, NK), jnp.int32),
            pltpu.VMEM((NW, 2, NO, NO), BF16),
            pltpu.SemaphoreType.DMA((5,)),
            pltpu.SemaphoreType.DMA,
            pltpu.SemaphoreType.DMA,
            pltpu.SemaphoreType.DMA,
            pltpu.SemaphoreType.DMA((2, CAP)),
            pltpu.SemaphoreType.DMA((slots,)),
            pltpu.SemaphoreType.DMA((slots,)),
            pltpu.SemaphoreType.DMA((slots,)),
        ],
        compiler_params=pltpu.CompilerParams(
            collective_id=0, has_side_effects=True, vmem_limit_bytes=48 * 1024 * 1024
        ),
    )(*operands)
    return result.reshape(green.shape)


def solution(mesh):
    placed = (P("energy", "mom", None, None), P(), P(), P(), P(), P())
    return jax.shard_map(
        body, mesh=mesh, in_specs=placed, out_specs=P("energy", "mom", None, None), check_vma=False
    )
```

```python
import jax
import jax.numpy as jnp
from jax import lax
from jax.experimental import pallas as pl
from jax.experimental.pallas import tpu as pltpu
from jax.sharding import PartitionSpec as P

MESH = pl.DeviceIdType.MESH
BF16 = jnp.bfloat16
F32 = jnp.float32

NO = 64
NW = 16
NK = 32
EB = 6
KB = 4
CHIPS = 4
PAIRS = 5
HALF = NO // 2
CHUNK = HALF // 2
PART = 2 * CHUNK
ROWS = 16
DEPTH = 3 * CHIPS * ROWS
TGT = 2 * KB * NW
OUT = 2 * KB * NO
RAWSTEP = 36
SHIFT = 4
ODD = TGT + 16
MIXSTEP = TGT + 8 + SHIFT
LINKS = ("up", "down")

UP = (
    (
        (1, 0, 0), (2, 0, 0), (3, 0, 0), (1, 0, 1), (2, 0, 1), (3, 0, 1), (4, 3, 0), (0, 3, 0),
        (4, 2, 0), (4, 2, 1), (4, 3, 1), (0, 2, 0), (0, 1, 0), (0, 3, 1), (4, 1, 0), (4, 1, 1),
        (0, 1, 1), (0, 2, 1),
    ),
    (
        (3, 1, 0), (3, 1, 1), (1, 1, 0), (1, 1, 1), (1, 0, 0), (2, 0, 0), (3, 0, 0), (1, 0, 1),
        (2, 1, 0), (3, 0, 1), (4, 3, 0), (0, 3, 0), (2, 0, 1), (2, 1, 1), (4, 3, 1), (), (),
        (0, 3, 1),
    ),
    (
        (1, 2, 0), (1, 2, 1), (3, 2, 0), (3, 2, 1), (3, 1, 0), (3, 1, 1), (1, 1, 0), (1, 1, 1),
        (1, 0, 0), (2, 2, 0), (3, 0, 0), (1, 0, 1), (2, 1, 0), (3, 0, 1), (2, 0, 0), (2, 2, 1),
        (2, 0, 1), (2, 1, 1),
    ),
    (
        (1, 3, 0), (1, 3, 1), (3, 3, 0), (3, 3, 1), (1, 2, 0), (1, 2, 1), (3, 2, 0), (3, 2, 1),
        (3, 1, 0), (3, 1, 1), (1, 1, 0), (1, 1, 1), (1, 0, 0), (), (3, 0, 0), (1, 0, 1), (),
        (3, 0, 1),
    ),
)
CAP = 4
EARLY = 4
LAG = 3
STEPS = max(len(row) for row in UP)


def up_target(chip, slot):
    pair, source = slot
    if chip < CHIPS - 1:
        return 0, chip + 1, slot
    return (1, 0, (0, source)) if pair == 3 else (-1, 0, (4, source))


def plan():
    out = [[[] for _ in range(STEPS)] for _ in range(CHIPS)]
    into = [[[] for _ in range(STEPS)] for _ in range(CHIPS)]
    for chip in range(CHIPS):
        for now, entry in enumerate(UP[chip]):
            if not entry:
                continue
            slot, chunk = entry[:2], entry[2]
            step, there, to = up_target(chip, slot)
            out[chip][now].append(("up", step, there, slot, to, chunk))
            into[there][now].append((to, chunk))
            far = [(PAIRS - 1 - s[0], CHIPS - 1 - s[1]) for s in (slot, to)]
            here, there = CHIPS - 1 - chip, CHIPS - 1 - there
            out[here][now].append(("down", -step, there, far[0], far[1], chunk))
            into[there][now].append((far[1], chunk))
    return out, into


def kernel(
    g_ref, occ_hbm, off_hbm, tc_hbm, idx_hbm, orb_hbm, out_ref,
    raw, spread_rows, buf, weights, odd_weights, left_mats, right_mats, mixed, sides,
    occ_ref, off_ref, tc_ref, idx_ref, orb_ref,
    small_sem, own_sem, raw_send, raw_recv, ici_send, ici_recv, sib_send, sib_recv,
):
    energies = lax.axis_size("energy")
    energy = lax.axis_index("energy")
    mom = lax.axis_index("mom")
    core = lax.rem(mom, 2)
    chip = lax.div(mom, 2)
    sibling = (energy, mom + 1 - 2 * core)
    outgoing, incoming = plan()
    late = max(now for rows in incoming for now, row in enumerate(rows) for _, c in row if c == 0)
    def device(step, there):
        return (lax.rem(energy + step + energies, energies), 2 * there + core)

    def partners(place):
        if place == 0:
            return [(1, CHIPS - 1), (-1, CHIPS - 1), (0, 1)]
        if place == CHIPS - 1:
            return [(1, 0), (-1, 0), (0, CHIPS - 2)]
        return [(0, place - 1), (0, place + 1)]

    def on_each_chip(act):
        for place in range(CHIPS):

            @pl.when(chip == place)
            def _(place=place):
                act(place)

    own = pltpu.make_async_copy(
        g_ref.at[:, :, pl.ds(core * HALF, HALF)], raw.at[core], own_sem
    )
    own.start()
    barrier = pltpu.get_barrier_semaphore()
    pl.semaphore_signal(barrier, inc=1, device_id=sibling, device_id_type=MESH)

    def greet(place):
        for step, there in partners(place):
            pl.semaphore_signal(
                barrier, inc=1, device_id=device(step, there), device_id_type=MESH
            )

    on_each_chip(greet)
    small = [
        pltpu.make_async_copy(a, b, small_sem.at[i])
        for i, (a, b) in enumerate(
            [
                (occ_hbm, occ_ref), (off_hbm, off_ref), (tc_hbm, tc_ref),
                (idx_hbm, idx_ref), (orb_hbm, orb_ref),
            ]
        )
    ]
    for copy in small:
        copy.start()
    on_each_chip(lambda place: pl.semaphore_wait(barrier, 1 + len(partners(place))))

    def raw_copy(side):
        return pltpu.make_async_remote_copy(
            src_ref=g_ref.at[:, :, pl.ds((1 - core) * HALF, HALF)],
            dst_ref=raw.at[side],
            send_sem=raw_send,
            recv_sem=raw_recv,
            device_id=sibling,
            device_id_type=MESH,
        )

    raw_copy(core).start()
    own.wait()
    raw_copy(1 - core).wait_recv()

    def turn(pairs):
        for pair in pairs:
            for e in range(2):
                for side in range(2):
                    for q in range(KB):
                        n = pair * ROWS + e * 8 + side * KB + q
                        spread_rows[pl.ds(n * RAWSTEP, HALF), :] = raw[
                            side, 2 * pair + e, q
                        ].astype(F32)

        def one(r, carry):
            for pair in pairs:
                rows = spread_rows[
                    pl.ds(pair * ROWS * RAWSTEP + r, ROWS, stride=RAWSTEP), :
                ]
                buf[pair + 1, chip, core * HALF + r] = rows.astype(BF16)
            return carry

        lax.fori_loop(0, HALF, one, 0, unroll=16)

    def rows_of(slot, side, chunk):
        return buf.at[slot[0], slot[1], pl.ds(side * HALF + chunk * CHUNK, CHUNK)]

    def number(slot, chunk):
        return (slot[0] * CHIPS + slot[1]) * 2 + chunk

    def ici_copy(now, link, step, there, slot, to, chunk):
        return pltpu.make_async_remote_copy(
            src_ref=rows_of(slot, core, chunk),
            dst_ref=rows_of(to, core, chunk),
            send_sem=ici_send.at[LINKS.index(link), now % CAP],
            recv_sem=ici_recv.at[number(to, chunk)],
            device_id=device(step, there),
            device_id_type=MESH,
        )

    def sib_copy(slot, chunk, side):
        return pltpu.make_async_remote_copy(
            src_ref=rows_of(slot, side, chunk),
            dst_ref=rows_of(slot, side, chunk),
            send_sem=sib_send.at[number(slot, chunk)],
            recv_sem=sib_recv.at[number(slot, chunk)],
            device_id=sibling,
            device_id_type=MESH,
        )

    got = [set() for _ in range(CHIPS)]

    def receive(place, chunks):
        for slot, chunk in chunks:
            if (slot, chunk) not in got[place]:
                got[place].add((slot, chunk))
                ici_copy(0, "up", 0, 0, slot, slot, chunk).wait_recv()
                sib_copy(slot, chunk, core).start()

    def steps(first, last):
        def act(place):
            for now in range(first, last):
                if CAP <= now < STEPS + CAP:
                    for copy in outgoing[place][now - CAP]:
                        ici_copy(now - CAP, *copy).wait_send()
                if now < STEPS:
                    for copy in outgoing[place][now]:
                        slot, chunk = copy[3], copy[5]
                        if slot[1] != place or slot[0] in (0, 4):
                            receive(place, [(slot, chunk)])
                        ici_copy(now, *copy).start()
                if LAG <= now < STEPS + LAG:
                    receive(place, incoming[place][now - LAG])

        on_each_chip(act)

    def from_sibling(chunk):
        for pair in range(PAIRS):
            for source in range(CHIPS):
                sib_copy((pair, source), chunk, 1 - core).wait_recv()

    outer_first = all(not c or c[0] != 2 for row in UP for c in row[:EARLY])
    turn((0, 2) if outer_first else (0, 1, 2))
    steps(0, EARLY)
    if outer_first:
        turn((1,))

    def own_to_sibling(place):
        for pair in (1, 2, 3):
            for chunk in range(2):
                sib_copy((pair, place), chunk, core).start()

    on_each_chip(own_to_sibling)
    for copy in small:
        copy.wait()

    column = lax.broadcasted_iota(jnp.int32, (NK, DEPTH), 1)
    source = lax.div(lax.rem(column, CHIPS * ROWS), ROWS) * 8 + lax.rem(column, 8)
    label = lax.broadcasted_iota(jnp.int32, (NK, DEPTH), 0)
    widen = (source == label).astype(F32).astype(BF16)
    target = lax.broadcasted_iota(jnp.int32, (8, NK), 0) + mom * KB
    pick = (target == lax.broadcasted_iota(jnp.int32, (8, NK), 1)).astype(F32).astype(BF16)
    table = idx_ref[...].astype(F32).astype(BF16)
    table = jnp.dot(pick, table, preferred_element_type=F32).astype(BF16)
    table = jnp.dot(table, widen, preferred_element_type=F32)
    mode = lax.broadcasted_iota(jnp.int32, (NW, DEPTH), 0)
    occ = jnp.zeros((NW, DEPTH), F32)
    off = jnp.zeros((NW, DEPTH), jnp.int32)
    for w in range(NW):
        occ = jnp.where(mode == w, occ_ref[w], occ)
        off = jnp.where(mode == w, off_ref[w], off)
    place_of = lax.broadcasted_iota(jnp.int32, (NW, DEPTH), 1)
    pair_of = lax.div(place_of, CHIPS * ROWS)
    energy_of = 2 * (pair_of - 1) + lax.div(lax.rem(place_of, ROWS), 8)
    first = (energy > 0).astype(F32)
    last = (energy < energies - 1).astype(F32)
    values = [[] for _ in range(2)]
    for k in range(KB):
        chosen = (table[k : k + 1, :] == label.astype(F32)).astype(F32).astype(BF16)
        spread = jnp.dot(tc_ref[...], chosen, preferred_element_type=F32)
        low = (occ * spread).astype(BF16).astype(F32)
        high = ((occ + 1.0) * spread).astype(BF16).astype(F32)
        for e in range(2):
            away = energy_of - e
            value = jnp.where(away < 0, low, high)
            values[e].append(jnp.where(jnp.abs(away) == off, value, 0.0))
    value = jnp.concatenate(values[0] + values[1], axis=0)
    pair_of = lax.div(lax.broadcasted_iota(jnp.int32, (TGT, DEPTH), 1), CHIPS * ROWS)
    for t, kept in ((0, first), (1, None), (2, last)):
        now = value if kept is None else jnp.where(pair_of == t, value * kept, value)
        weights[t] = now.astype(BF16)
        above = jnp.zeros((SHIFT, DEPTH), F32)
        below = jnp.zeros((ODD - TGT - SHIFT, DEPTH), F32)
        odd_weights[t] = jnp.concatenate([above, now, below], axis=0).astype(BF16)

    here = lax.broadcasted_iota(jnp.int32, (128, 128), 1)
    row = lax.rem(here, PART)
    wanted = lax.div(lax.rem(here, 2 * PART), PART) * NO + lax.div(here, 2 * PART) * CHUNK
    wanted = wanted + lax.div(row, CHUNK) * HALF + lax.rem(row, CHUNK)
    apart = (wanted == lax.broadcasted_iota(jnp.int32, (128, 128), 0)).astype(F32).astype(BF16)
    right_mats[...] = jnp.zeros_like(right_mats)
    for i in range(NW // 2):
        moved = []
        for h in range(2):
            real = orb_ref[2 * i + h, 0].astype(F32)
            imag = orb_ref[2 * i + h, 1].astype(F32)
            top = jnp.concatenate([real, imag], axis=1)
            bottom = jnp.concatenate([-imag, real], axis=1)
            block = jnp.concatenate([top, bottom], axis=0).T.astype(BF16)
            right_mats[i, pl.ds(h * 128, 128), pl.ds(h * 128, 128)] = block
            moved.append(jnp.dot(top.astype(BF16), apart, preferred_element_type=F32))
        for part in range(2):
            columns = slice(part * 2 * PART, (part + 1) * 2 * PART)
            pair = jnp.concatenate([m[:, columns] for m in moved], axis=1)
            left_mats[part, :, pl.ds(i * 128, 128)] = pair.astype(BF16)

    def mix(side, chunk):
        base = side * HALF + chunk * CHUNK

        def one(t, carry):
            for i in range(CHUNK // 4):
                for odd, matrix in enumerate((weights, odd_weights)):
                    wide = []
                    for r in (4 * i + odd, 4 * i + odd + 2):
                        parts = [buf[t + p, s, base + r] for p in range(3) for s in range(CHIPS)]
                        wide.append(jnp.concatenate(parts, axis=0))
                    got = jnp.dot(
                        matrix[t], jnp.concatenate(wide, axis=1), preferred_element_type=F32
                    )
                    start = (t * PART + side * CHUNK + 4 * i) * MIXSTEP + odd * (MIXSTEP - SHIFT)
                    mixed[pl.ds(pl.multiple_of(start, 8), matrix.shape[1]), :] = got[:, :128]
                    start = start + 2 * MIXSTEP
                    mixed[pl.ds(pl.multiple_of(start, 8), matrix.shape[1]), :] = got[:, 128:]
            return carry

        lax.fori_loop(0, 3, one, 0)

    def modes(part, t):
        for i in range(NW // 2):
            pair = []
            for w in (2 * i, 2 * i + 1):
                rows = []
                for n in range(2 * KB):
                    start = t * (PART * MIXSTEP) + n * NW + w
                    rows.append(mixed[pl.ds(start, PART, stride=MIXSTEP), :].astype(BF16))
                pair.append(jnp.concatenate(rows, axis=0))
            got = jnp.dot(
                jnp.concatenate(pair, axis=1), right_mats[i], preferred_element_type=F32
            ).astype(BF16)
            for h in range(2):
                depth = (2 * i + h) * 2 * PART
                y = got[:, h * 128 : (h + 1) * 128]
                turned = jnp.concatenate([-y[:, NO:], y[:, :NO]], axis=1)
                for n in range(2 * KB):
                    rows = slice(n * PART, (n + 1) * PART)
                    sides[n, pl.ds(depth, PART), :] = y[rows]
                    sides[n, pl.ds(depth + PART, PART), :] = turned[rows]
        for j in range(KB):
            both = jnp.concatenate([sides[2 * j], sides[2 * j + 1]], axis=1)
            got = jnp.dot(left_mats[part], both, preferred_element_type=F32)
            for h in range(2):
                rows = pl.ds(pl.multiple_of(t * OUT + (2 * j + h) * NO, NO), NO)
                value = got[:, h * 128 : (h + 1) * 128]
                if part == 0:
                    out_ref[rows, :] = value
                else:
                    out_ref[rows, :] += value

    now = late + LAG + 1
    steps(EARLY, now)
    mix(core, 0)
    steps(now, now + 1)
    from_sibling(0)
    mix(1 - core, 0)
    steps(now + 1, now + 2)
    for t in range(3):
        modes(0, t)
        steps(now + 2 + t, now + 3 + t)
    steps(now + 5, STEPS + max(CAP, LAG))
    mix(core, 1)
    from_sibling(1)
    mix(1 - core, 1)

    def second(t, carry):
        modes(1, t)
        return carry

    lax.fori_loop(0, 3, second, 0)

    raw_copy(core).wait_send()

    def finish(place):
        for slot in [(p, s) for p in range(PAIRS) for s in range(CHIPS)]:
            for chunk in range(2):
                sib_copy(slot, chunk, core).wait_send()

    finish(0)


def body(green, occupation, coupling, orbital, offsets, index):
    hbm = pl.BlockSpec(memory_space=pltpu.HBM)
    operands = [
        pltpu.with_memory_space_constraint(a, pltpu.HBM)
        for a in (green, occupation, offsets, coupling, index, orbital)
    ]
    slots = PAIRS * CHIPS * 2
    result = pl.pallas_call(
        kernel,
        out_shape=jax.ShapeDtypeStruct((3 * OUT, 128), F32),
        in_specs=[hbm] * 6,
        out_specs=pl.BlockSpec(memory_space=pltpu.VMEM),
        scratch_shapes=[
            pltpu.VMEM((2, EB, KB, HALF, 128), BF16),
            pltpu.VMEM((3 * ROWS * RAWSTEP, 128), F32),
            pltpu.VMEM((PAIRS, CHIPS, NO, ROWS, 128), BF16),
            pltpu.VMEM((3, TGT, DEPTH), BF16),
            pltpu.VMEM((3, ODD, DEPTH), BF16),
            pltpu.VMEM((2, NO, NW * 2 * PART), BF16),
            pltpu.VMEM((NW // 2, 256, 256), BF16),
            pltpu.VMEM((3 * PART * MIXSTEP, 128), F32),
            pltpu.VMEM((2 * KB, NW * 2 * PART, 128), BF16),
            pltpu.SMEM((NW,), F32),
            pltpu.SMEM((NW,), jnp.int32),
            pltpu.VMEM((NW, NK), BF16),
            pltpu.VMEM((NK, NK), jnp.int32),
            pltpu.VMEM((NW, 2, NO, NO), BF16),
            pltpu.SemaphoreType.DMA((5,)),
            pltpu.SemaphoreType.DMA,
            pltpu.SemaphoreType.DMA,
            pltpu.SemaphoreType.DMA,
            pltpu.SemaphoreType.DMA((2, CAP)),
            pltpu.SemaphoreType.DMA((slots,)),
            pltpu.SemaphoreType.DMA((slots,)),
            pltpu.SemaphoreType.DMA((slots,)),
        ],
        compiler_params=pltpu.CompilerParams(
            collective_id=0, has_side_effects=True, vmem_limit_bytes=48 * 1024 * 1024
        ),
    )(*operands)
    return result.reshape(green.shape)


def solution(mesh):
    placed = (P("energy", "mom", None, None), P(), P(), P(), P(), P())
    return jax.shard_map(
        body, mesh=mesh, in_specs=placed, out_specs=P("energy", "mom", None, None), check_vma=False
    )
```

```python
import jax
import jax.numpy as jnp
from jax import lax
from jax.experimental import pallas as pl
from jax.experimental.pallas import tpu as pltpu
from jax.sharding import PartitionSpec as P

MESH = pl.DeviceIdType.MESH
BF16 = jnp.bfloat16
F32 = jnp.float32

NO = 64
NW = 16
NK = 32
EB = 6
KB = 4
CHIPS = 4
PAIRS = 5
HALF = NO // 2
CHUNK = HALF // 2
PART = 2 * CHUNK
ROWS = 16
DEPTH = 3 * CHIPS * ROWS
TGT = 2 * KB * NW
OUT = 2 * KB * NO
RAWSTEP = 36
SHIFT = 4
ODD = TGT + 16
MIXSTEP = TGT + 8 + SHIFT
LINKS = ("up", "down")

UP = (
    (
        (1, 0, 0), (3, 0, 0), (2, 0, 0), (1, 0, 1), (3, 0, 1), (4, 3, 0), (0, 3, 0), (2, 0, 1),
        (4, 2, 0), (0, 2, 0), (4, 3, 1), (0, 3, 1), (0, 1, 0), (4, 1, 0), (0, 1, 1), (4, 1, 1),
        (4, 2, 1), (0, 2, 1),
    ),
    (
        (3, 1, 0), (1, 1, 0), (3, 1, 1), (1, 1, 1), (1, 0, 0), (3, 0, 0), (2, 0, 0), (1, 0, 1),
        (3, 0, 1), (4, 3, 0), (2, 1, 0), (2, 0, 1), (0, 3, 0), (2, 1, 1), (4, 3, 1), (0, 3, 1),
    ),
    (
        (1, 2, 0), (3, 2, 0), (1, 2, 1), (3, 2, 1), (3, 1, 0), (1, 1, 0), (3, 1, 1), (1, 1, 1),
        (1, 0, 0), (3, 0, 0), (2, 0, 0), (1, 0, 1), (2, 2, 0), (3, 0, 1), (2, 1, 0), (2, 0, 1),
        (2, 2, 1), (2, 1, 1),
    ),
    (
        (3, 3, 0), (1, 3, 0), (3, 3, 1), (1, 3, 1), (1, 2, 0), (3, 2, 0), (1, 2, 1), (3, 2, 1),
        (3, 1, 0), (1, 1, 0), (3, 1, 1), (1, 1, 1), (1, 0, 0), (3, 0, 0), (), (1, 0, 1), (),
        (3, 0, 1),
    ),
)
CAP = 4
EARLY = 4
LAG = 4
STEPS = max(len(row) for row in UP)


def up_target(chip, slot):
    pair, source = slot
    if chip < CHIPS - 1:
        return 0, chip + 1, slot
    return (1, 0, (0, source)) if pair == 3 else (-1, 0, (4, source))


def plan():
    out = [[[] for _ in range(STEPS)] for _ in range(CHIPS)]
    into = [[[] for _ in range(STEPS)] for _ in range(CHIPS)]
    for chip in range(CHIPS):
        for now, entry in enumerate(UP[chip]):
            if not entry:
                continue
            slot, chunk = entry[:2], entry[2]
            step, there, to = up_target(chip, slot)
            out[chip][now].append(("up", step, there, slot, to, chunk))
            into[there][now].append((to, chunk))
            far = [(PAIRS - 1 - s[0], CHIPS - 1 - s[1]) for s in (slot, to)]
            here, there = CHIPS - 1 - chip, CHIPS - 1 - there
            out[here][now].append(("down", -step, there, far[0], far[1], chunk))
            into[there][now].append((far[1], chunk))
    return out, into


def kernel(
    g_ref, occ_hbm, off_hbm, tc_hbm, idx_hbm, orb_hbm, out_ref,
    raw, spread_rows, buf, weights, odd_weights, left_mats, right_mats, mixed, sides,
    occ_ref, off_ref, tc_ref, idx_ref, orb_ref,
    small_sem, own_sem, raw_send, raw_recv, ici_send, ici_recv, sib_send, sib_recv,
):
    energies = lax.axis_size("energy")
    energy = lax.axis_index("energy")
    mom = lax.axis_index("mom")
    core = lax.rem(mom, 2)
    chip = lax.div(mom, 2)
    sibling = (energy, mom + 1 - 2 * core)
    outgoing, incoming = plan()
    late = max(now for rows in incoming for now, row in enumerate(rows) for _, c in row if c == 0)
    def device(step, there):
        return (lax.rem(energy + step + energies, energies), 2 * there + core)

    def partners(place):
        if place == 0:
            return [(1, CHIPS - 1), (-1, CHIPS - 1), (0, 1)]
        if place == CHIPS - 1:
            return [(1, 0), (-1, 0), (0, CHIPS - 2)]
        return [(0, place - 1), (0, place + 1)]

    def on_each_chip(act):
        for place in range(CHIPS):

            @pl.when(chip == place)
            def _(place=place):
                act(place)

    own = pltpu.make_async_copy(
        g_ref.at[:, :, pl.ds(core * HALF, HALF)], raw.at[core], own_sem
    )
    own.start()
    barrier = pltpu.get_barrier_semaphore()
    pl.semaphore_signal(barrier, inc=1, device_id=sibling, device_id_type=MESH)

    def greet(place):
        for step, there in partners(place):
            pl.semaphore_signal(
                barrier, inc=1, device_id=device(step, there), device_id_type=MESH
            )

    on_each_chip(greet)
    small = [
        pltpu.make_async_copy(a, b, small_sem.at[i])
        for i, (a, b) in enumerate(
            [
                (occ_hbm, occ_ref), (off_hbm, off_ref), (tc_hbm, tc_ref),
                (idx_hbm, idx_ref), (orb_hbm, orb_ref),
            ]
        )
    ]
    for copy in small:
        copy.start()
    on_each_chip(lambda place: pl.semaphore_wait(barrier, 1 + len(partners(place))))

    def raw_copy(side):
        return pltpu.make_async_remote_copy(
            src_ref=g_ref.at[:, :, pl.ds((1 - core) * HALF, HALF)],
            dst_ref=raw.at[side],
            send_sem=raw_send,
            recv_sem=raw_recv,
            device_id=sibling,
            device_id_type=MESH,
        )

    raw_copy(core).start()
    own.wait()
    raw_copy(1 - core).wait_recv()

    def turn(pairs):
        for pair in pairs:
            for e in range(2):
                for side in range(2):
                    for q in range(KB):
                        n = pair * ROWS + e * 8 + side * KB + q
                        spread_rows[pl.ds(n * RAWSTEP, HALF), :] = raw[
                            side, 2 * pair + e, q
                        ].astype(F32)

        def one(r, carry):
            for pair in pairs:
                rows = spread_rows[
                    pl.ds(pair * ROWS * RAWSTEP + r, ROWS, stride=RAWSTEP), :
                ]
                buf[pair + 1, chip, core * HALF + r] = rows.astype(BF16)
            return carry

        lax.fori_loop(0, HALF, one, 0, unroll=16)

    def rows_of(slot, side, chunk):
        return buf.at[slot[0], slot[1], pl.ds(side * HALF + chunk * CHUNK, CHUNK)]

    def number(slot, chunk):
        return (slot[0] * CHIPS + slot[1]) * 2 + chunk

    def ici_copy(now, link, step, there, slot, to, chunk):
        return pltpu.make_async_remote_copy(
            src_ref=rows_of(slot, core, chunk),
            dst_ref=rows_of(to, core, chunk),
            send_sem=ici_send.at[LINKS.index(link), now % CAP],
            recv_sem=ici_recv.at[number(to, chunk)],
            device_id=device(step, there),
            device_id_type=MESH,
        )

    def sib_copy(slot, chunk, side):
        return pltpu.make_async_remote_copy(
            src_ref=rows_of(slot, side, chunk),
            dst_ref=rows_of(slot, side, chunk),
            send_sem=sib_send.at[number(slot, chunk)],
            recv_sem=sib_recv.at[number(slot, chunk)],
            device_id=sibling,
            device_id_type=MESH,
        )

    got = [set() for _ in range(CHIPS)]

    def receive(place, chunks):
        for slot, chunk in chunks:
            if (slot, chunk) not in got[place]:
                got[place].add((slot, chunk))
                ici_copy(0, "up", 0, 0, slot, slot, chunk).wait_recv()
                sib_copy(slot, chunk, core).start()

    def steps(first, last):
        def act(place):
            for now in range(first, last):
                if CAP <= now < STEPS + CAP:
                    for copy in outgoing[place][now - CAP]:
                        ici_copy(now - CAP, *copy).wait_send()
                if now < STEPS:
                    for copy in outgoing[place][now]:
                        slot, chunk = copy[3], copy[5]
                        if slot[1] != place or slot[0] in (0, 4):
                            receive(place, [(slot, chunk)])
                        ici_copy(now, *copy).start()
                if LAG <= now < STEPS + LAG:
                    receive(place, incoming[place][now - LAG])

        on_each_chip(act)

    def from_sibling(chunk):
        for pair in range(PAIRS):
            for source in range(CHIPS):
                sib_copy((pair, source), chunk, 1 - core).wait_recv()

    outer_first = all(not c or c[0] != 2 for row in UP for c in row[:EARLY])
    turn((0, 2) if outer_first else (0, 1, 2))
    steps(0, EARLY)
    if outer_first:
        turn((1,))

    def own_to_sibling(place):
        for pair in (1, 2, 3):
            for chunk in range(2):
                sib_copy((pair, place), chunk, core).start()

    on_each_chip(own_to_sibling)
    for copy in small:
        copy.wait()

    column = lax.broadcasted_iota(jnp.int32, (NK, DEPTH), 1)
    source = lax.div(lax.rem(column, CHIPS * ROWS), ROWS) * 8 + lax.rem(column, 8)
    label = lax.broadcasted_iota(jnp.int32, (NK, DEPTH), 0)
    widen = (source == label).astype(F32).astype(BF16)
    target = lax.broadcasted_iota(jnp.int32, (8, NK), 0) + mom * KB
    pick = (target == lax.broadcasted_iota(jnp.int32, (8, NK), 1)).astype(F32).astype(BF16)
    table = idx_ref[...].astype(F32).astype(BF16)
    table = jnp.dot(pick, table, preferred_element_type=F32).astype(BF16)
    table = jnp.dot(table, widen, preferred_element_type=F32)
    mode = lax.broadcasted_iota(jnp.int32, (NW, DEPTH), 0)
    occ = jnp.zeros((NW, DEPTH), F32)
    off = jnp.zeros((NW, DEPTH), jnp.int32)
    for w in range(NW):
        occ = jnp.where(mode == w, occ_ref[w], occ)
        off = jnp.where(mode == w, off_ref[w], off)
    place_of = lax.broadcasted_iota(jnp.int32, (NW, DEPTH), 1)
    pair_of = lax.div(place_of, CHIPS * ROWS)
    energy_of = 2 * (pair_of - 1) + lax.div(lax.rem(place_of, ROWS), 8)
    first = (energy > 0).astype(F32)
    last = (energy < energies - 1).astype(F32)
    values = [[] for _ in range(2)]
    for k in range(KB):
        chosen = (table[k : k + 1, :] == label.astype(F32)).astype(F32).astype(BF16)
        spread = jnp.dot(tc_ref[...], chosen, preferred_element_type=F32)
        low = (occ * spread).astype(BF16).astype(F32)
        high = ((occ + 1.0) * spread).astype(BF16).astype(F32)
        for e in range(2):
            away = energy_of - e
            value = jnp.where(away < 0, low, high)
            values[e].append(jnp.where(jnp.abs(away) == off, value, 0.0))
    value = jnp.concatenate(values[0] + values[1], axis=0)
    pair_of = lax.div(lax.broadcasted_iota(jnp.int32, (TGT, DEPTH), 1), CHIPS * ROWS)
    for t, kept in ((0, first), (1, None), (2, last)):
        now = value if kept is None else jnp.where(pair_of == t, value * kept, value)
        weights[t] = now.astype(BF16)
        above = jnp.zeros((SHIFT, DEPTH), F32)
        below = jnp.zeros((ODD - TGT - SHIFT, DEPTH), F32)
        odd_weights[t] = jnp.concatenate([above, now, below], axis=0).astype(BF16)

    here = lax.broadcasted_iota(jnp.int32, (128, 128), 1)
    row = lax.rem(here, PART)
    wanted = lax.div(lax.rem(here, 2 * PART), PART) * NO + lax.div(here, 2 * PART) * CHUNK
    wanted = wanted + lax.div(row, CHUNK) * HALF + lax.rem(row, CHUNK)
    apart = (wanted == lax.broadcasted_iota(jnp.int32, (128, 128), 0)).astype(F32).astype(BF16)
    right_mats[...] = jnp.zeros_like(right_mats)
    for i in range(NW // 2):
        moved = []
        for h in range(2):
            real = orb_ref[2 * i + h, 0].astype(F32)
            imag = orb_ref[2 * i + h, 1].astype(F32)
            top = jnp.concatenate([real, imag], axis=1)
            bottom = jnp.concatenate([-imag, real], axis=1)
            block = jnp.concatenate([top, bottom], axis=0).T.astype(BF16)
            right_mats[i, pl.ds(h * 128, 128), pl.ds(h * 128, 128)] = block
            moved.append(jnp.dot(top.astype(BF16), apart, preferred_element_type=F32))
        for part in range(2):
            columns = slice(part * 2 * PART, (part + 1) * 2 * PART)
            pair = jnp.concatenate([m[:, columns] for m in moved], axis=1)
            left_mats[part, :, pl.ds(i * 128, 128)] = pair.astype(BF16)

    def mix(side, chunk):
        base = side * HALF + chunk * CHUNK

        def one(t, carry):
            for i in range(CHUNK // 4):
                for odd, matrix in enumerate((weights, odd_weights)):
                    wide = []
                    for r in (4 * i + odd, 4 * i + odd + 2):
                        parts = [buf[t + p, s, base + r] for p in range(3) for s in range(CHIPS)]
                        wide.append(jnp.concatenate(parts, axis=0))
                    got = jnp.dot(
                        matrix[t], jnp.concatenate(wide, axis=1), preferred_element_type=F32
                    )
                    start = (t * PART + side * CHUNK + 4 * i) * MIXSTEP + odd * (MIXSTEP - SHIFT)
                    mixed[pl.ds(pl.multiple_of(start, 8), matrix.shape[1]), :] = got[:, :128]
                    start = start + 2 * MIXSTEP
                    mixed[pl.ds(pl.multiple_of(start, 8), matrix.shape[1]), :] = got[:, 128:]
            return carry

        lax.fori_loop(0, 3, one, 0)

    def modes(part, t):
        for i in range(NW // 2):
            pair = []
            for w in (2 * i, 2 * i + 1):
                rows = []
                for n in range(2 * KB):
                    start = t * (PART * MIXSTEP) + n * NW + w
                    rows.append(mixed[pl.ds(start, PART, stride=MIXSTEP), :].astype(BF16))
                pair.append(jnp.concatenate(rows, axis=0))
            got = jnp.dot(
                jnp.concatenate(pair, axis=1), right_mats[i], preferred_element_type=F32
            ).astype(BF16)
            for h in range(2):
                depth = (2 * i + h) * 2 * PART
                y = got[:, h * 128 : (h + 1) * 128]
                turned = jnp.concatenate([-y[:, NO:], y[:, :NO]], axis=1)
                for n in range(2 * KB):
                    rows = slice(n * PART, (n + 1) * PART)
                    sides[n, pl.ds(depth, PART), :] = y[rows]
                    sides[n, pl.ds(depth + PART, PART), :] = turned[rows]
        for j in range(KB):
            both = jnp.concatenate([sides[2 * j], sides[2 * j + 1]], axis=1)
            got = jnp.dot(left_mats[part], both, preferred_element_type=F32)
            for h in range(2):
                rows = pl.ds(pl.multiple_of(t * OUT + (2 * j + h) * NO, NO), NO)
                value = got[:, h * 128 : (h + 1) * 128]
                if part == 0:
                    out_ref[rows, :] = value
                else:
                    out_ref[rows, :] += value

    now = late + LAG
    steps(EARLY, now)
    on_each_chip(
        lambda place: receive(place, [c for row in incoming[place] for c in row if c[1] == 0])
    )
    mix(core, 0)
    steps(now, now + 1)
    from_sibling(0)
    mix(1 - core, 0)
    steps(now + 1, now + 2)
    for t in range(3):
        modes(0, t)
        steps(now + 2 + t, now + 3 + t)
    steps(now + 5, STEPS + max(CAP, LAG))
    mix(core, 1)
    from_sibling(1)
    mix(1 - core, 1)

    def second(t, carry):
        modes(1, t)
        return carry

    lax.fori_loop(0, 3, second, 0)

    raw_copy(core).wait_send()

    def finish(place):
        for slot in [(p, s) for p in range(PAIRS) for s in range(CHIPS)]:
            for chunk in range(2):
                sib_copy(slot, chunk, core).wait_send()

    finish(0)


def body(green, occupation, coupling, orbital, offsets, index):
    hbm = pl.BlockSpec(memory_space=pltpu.HBM)
    operands = [
        pltpu.with_memory_space_constraint(a, pltpu.HBM)
        for a in (green, occupation, offsets, coupling, index, orbital)
    ]
    slots = PAIRS * CHIPS * 2
    result = pl.pallas_call(
        kernel,
        out_shape=jax.ShapeDtypeStruct((3 * OUT, 128), F32),
        in_specs=[hbm] * 6,
        out_specs=pl.BlockSpec(memory_space=pltpu.VMEM),
        scratch_shapes=[
            pltpu.VMEM((2, EB, KB, HALF, 128), BF16),
            pltpu.VMEM((3 * ROWS * RAWSTEP, 128), F32),
            pltpu.VMEM((PAIRS, CHIPS, NO, ROWS, 128), BF16),
            pltpu.VMEM((3, TGT, DEPTH), BF16),
            pltpu.VMEM((3, ODD, DEPTH), BF16),
            pltpu.VMEM((2, NO, NW * 2 * PART), BF16),
            pltpu.VMEM((NW // 2, 256, 256), BF16),
            pltpu.VMEM((3 * PART * MIXSTEP, 128), F32),
            pltpu.VMEM((2 * KB, NW * 2 * PART, 128), BF16),
            pltpu.SMEM((NW,), F32),
            pltpu.SMEM((NW,), jnp.int32),
            pltpu.VMEM((NW, NK), BF16),
            pltpu.VMEM((NK, NK), jnp.int32),
            pltpu.VMEM((NW, 2, NO, NO), BF16),
            pltpu.SemaphoreType.DMA((5,)),
            pltpu.SemaphoreType.DMA,
            pltpu.SemaphoreType.DMA,
            pltpu.SemaphoreType.DMA,
            pltpu.SemaphoreType.DMA((2, CAP)),
            pltpu.SemaphoreType.DMA((slots,)),
            pltpu.SemaphoreType.DMA((slots,)),
            pltpu.SemaphoreType.DMA((slots,)),
        ],
        compiler_params=pltpu.CompilerParams(
            collective_id=0, has_side_effects=True, vmem_limit_bytes=48 * 1024 * 1024
        ),
    )(*operands)
    return result.reshape(green.shape)


def solution(mesh):
    placed = (P("energy", "mom", None, None), P(), P(), P(), P(), P())
    return jax.shard_map(
        body, mesh=mesh, in_specs=placed, out_specs=P("energy", "mom", None, None), check_vma=False
    )
```

```python
import jax
import jax.numpy as jnp
from jax import lax
from jax.experimental import pallas as pl
from jax.experimental.pallas import tpu as pltpu
from jax.sharding import PartitionSpec as P

MESH = pl.DeviceIdType.MESH
BF16 = jnp.bfloat16
F32 = jnp.float32

NO = 64
NW = 16
NK = 32
EB = 6
KB = 4
CHIPS = 4
PAIRS = 5
HALF = NO // 2
CHUNK = HALF // 2
PART = 2 * CHUNK
ROWS = 16
DEPTH = 3 * CHIPS * ROWS
TGT = 2 * KB * NW
OUT = 2 * KB * NO
RAWSTEP = 36
SHIFT = 4
ODD = TGT + 16
MIXSTEP = TGT + 8 + SHIFT
LINKS = ("up", "down")

UP = (
    (
        (1, 0, 0), (3, 0, 0), (2, 0, 0), (1, 0, 1), (3, 0, 1), (4, 3, 0), (0, 3, 0), (2, 0, 1),
        (4, 2, 0), (0, 2, 0), (4, 3, 1), (0, 3, 1), (0, 1, 0), (4, 1, 0), (0, 1, 1), (4, 1, 1),
        (4, 2, 1), (0, 2, 1),
    ),
    (
        (3, 1, 0), (1, 1, 0), (3, 1, 1), (1, 1, 1), (1, 0, 0), (3, 0, 0), (2, 0, 0), (1, 0, 1),
        (3, 0, 1), (4, 3, 0), (2, 1, 0), (2, 0, 1), (0, 3, 0), (2, 1, 1), (4, 3, 1), (0, 3, 1),
    ),
    (
        (1, 2, 0), (3, 2, 0), (1, 2, 1), (3, 2, 1), (3, 1, 0), (1, 1, 0), (3, 1, 1), (1, 1, 1),
        (1, 0, 0), (3, 0, 0), (2, 0, 0), (1, 0, 1), (2, 2, 0), (3, 0, 1), (2, 1, 0), (2, 0, 1),
        (2, 2, 1), (2, 1, 1),
    ),
    (
        (3, 3, 0), (1, 3, 0), (3, 3, 1), (1, 3, 1), (1, 2, 0), (3, 2, 0), (1, 2, 1), (3, 2, 1),
        (3, 1, 0), (1, 1, 0), (3, 1, 1), (1, 1, 1), (1, 0, 0), (3, 0, 0), (), (1, 0, 1), (),
        (3, 0, 1),
    ),
)
CAP = 4
EARLY = 4
LAG = 4
STEPS = max(len(row) for row in UP)


def up_target(chip, slot):
    pair, source = slot
    if chip < CHIPS - 1:
        return 0, chip + 1, slot
    return (1, 0, (0, source)) if pair == 3 else (-1, 0, (4, source))


def plan():
    out = [[[] for _ in range(STEPS)] for _ in range(CHIPS)]
    into = [[[] for _ in range(STEPS)] for _ in range(CHIPS)]
    for chip in range(CHIPS):
        for now, entry in enumerate(UP[chip]):
            if not entry:
                continue
            slot, chunk = entry[:2], entry[2]
            step, there, to = up_target(chip, slot)
            out[chip][now].append(("up", step, there, slot, to, chunk))
            into[there][now].append((to, chunk))
            far = [(PAIRS - 1 - s[0], CHIPS - 1 - s[1]) for s in (slot, to)]
            here, there = CHIPS - 1 - chip, CHIPS - 1 - there
            out[here][now].append(("down", -step, there, far[0], far[1], chunk))
            into[there][now].append((far[1], chunk))
    return out, into


def kernel(
    g_ref, occ_hbm, off_hbm, tc_hbm, idx_hbm, orb_hbm, out_ref,
    raw, spread_rows, buf, weights, odd_weights, left_mats, right_mats, mixed, sides,
    occ_ref, off_ref, tc_ref, idx_ref, orb_ref,
    small_sem, own_sem, raw_send, raw_recv, ici_send, ici_recv, sib_send, sib_recv,
):
    energies = lax.axis_size("energy")
    energy = lax.axis_index("energy")
    mom = lax.axis_index("mom")
    core = lax.rem(mom, 2)
    chip = lax.div(mom, 2)
    sibling = (energy, mom + 1 - 2 * core)
    outgoing, incoming = plan()
    late = max(now for rows in incoming for now, row in enumerate(rows) for _, c in row if c == 0)
    def device(step, there):
        return (lax.rem(energy + step + energies, energies), 2 * there + core)

    def partners(place):
        if place == 0:
            return [(1, CHIPS - 1), (-1, CHIPS - 1), (0, 1)]
        if place == CHIPS - 1:
            return [(1, 0), (-1, 0), (0, CHIPS - 2)]
        return [(0, place - 1), (0, place + 1)]

    def on_each_chip(act):
        for place in range(CHIPS):

            @pl.when(chip == place)
            def _(place=place):
                act(place)

    own = pltpu.make_async_copy(
        g_ref.at[:, :, pl.ds(core * HALF, HALF)], raw.at[core], own_sem
    )
    own.start()
    barrier = pltpu.get_barrier_semaphore()
    pl.semaphore_signal(barrier, inc=1, device_id=sibling, device_id_type=MESH)

    def greet(place):
        for step, there in partners(place):
            pl.semaphore_signal(
                barrier, inc=1, device_id=device(step, there), device_id_type=MESH
            )

    on_each_chip(greet)
    small = [
        pltpu.make_async_copy(a, b, small_sem.at[i])
        for i, (a, b) in enumerate(
            [
                (occ_hbm, occ_ref), (off_hbm, off_ref), (tc_hbm, tc_ref),
                (idx_hbm, idx_ref), (orb_hbm, orb_ref),
            ]
        )
    ]
    for copy in small:
        copy.start()
    on_each_chip(lambda place: pl.semaphore_wait(barrier, 1 + len(partners(place))))

    def raw_copy(side):
        return pltpu.make_async_remote_copy(
            src_ref=g_ref.at[:, :, pl.ds((1 - core) * HALF, HALF)],
            dst_ref=raw.at[side],
            send_sem=raw_send,
            recv_sem=raw_recv,
            device_id=sibling,
            device_id_type=MESH,
        )

    raw_copy(core).start()
    own.wait()
    raw_copy(1 - core).wait_recv()

    def turn(pairs):
        for pair in pairs:
            for e in range(2):
                for side in range(2):
                    for q in range(KB):
                        n = pair * ROWS + e * 8 + side * KB + q
                        spread_rows[pl.ds(n * RAWSTEP, HALF), :] = raw[
                            side, 2 * pair + e, q
                        ].astype(F32)

        def one(r, carry):
            for pair in pairs:
                rows = spread_rows[
                    pl.ds(pair * ROWS * RAWSTEP + r, ROWS, stride=RAWSTEP), :
                ]
                buf[pair + 1, chip, core * HALF + r] = rows.astype(BF16)
            return carry

        lax.fori_loop(0, HALF, one, 0, unroll=16)

    def rows_of(slot, side, chunk):
        return buf.at[slot[0], slot[1], pl.ds(side * HALF + chunk * CHUNK, CHUNK)]

    def number(slot, chunk):
        return (slot[0] * CHIPS + slot[1]) * 2 + chunk

    def ici_copy(now, link, step, there, slot, to, chunk):
        return pltpu.make_async_remote_copy(
            src_ref=rows_of(slot, core, chunk),
            dst_ref=rows_of(to, core, chunk),
            send_sem=ici_send.at[LINKS.index(link), now % CAP],
            recv_sem=ici_recv.at[number(to, chunk)],
            device_id=device(step, there),
            device_id_type=MESH,
        )

    def sib_copy(slot, chunk, side):
        return pltpu.make_async_remote_copy(
            src_ref=rows_of(slot, side, chunk),
            dst_ref=rows_of(slot, side, chunk),
            send_sem=sib_send.at[number(slot, chunk)],
            recv_sem=sib_recv.at[number(slot, chunk)],
            device_id=sibling,
            device_id_type=MESH,
        )

    got = [set() for _ in range(CHIPS)]

    def receive(place, chunks):
        for slot, chunk in chunks:
            if (slot, chunk) not in got[place]:
                got[place].add((slot, chunk))
                ici_copy(0, "up", 0, 0, slot, slot, chunk).wait_recv()
                sib_copy(slot, chunk, core).start()

    def steps(first, last):
        def act(place):
            for now in range(first, last):
                if CAP <= now < STEPS + CAP:
                    for copy in outgoing[place][now - CAP]:
                        ici_copy(now - CAP, *copy).wait_send()
                if now < STEPS:
                    for copy in outgoing[place][now]:
                        slot, chunk = copy[3], copy[5]
                        if slot[1] != place or slot[0] in (0, 4):
                            receive(place, [(slot, chunk)])
                        ici_copy(now, *copy).start()
                if LAG <= now < STEPS + LAG:
                    receive(place, incoming[place][now - LAG])

        on_each_chip(act)

    def from_sibling(chunk):
        for pair in range(PAIRS):
            for source in range(CHIPS):
                sib_copy((pair, source), chunk, 1 - core).wait_recv()

    outer_first = all(not c or c[0] != 2 for row in UP for c in row[:EARLY])
    turn((0, 2) if outer_first else (0, 1, 2))
    steps(0, EARLY)
    if outer_first:
        turn((1,))

    def own_to_sibling(place):
        for pair in (1, 2, 3):
            for chunk in range(2):
                sib_copy((pair, place), chunk, core).start()

    on_each_chip(own_to_sibling)
    for copy in small:
        copy.wait()

    column = lax.broadcasted_iota(jnp.int32, (NK, DEPTH), 1)
    source = lax.div(lax.rem(column, CHIPS * ROWS), ROWS) * 8 + lax.rem(column, 8)
    label = lax.broadcasted_iota(jnp.int32, (NK, DEPTH), 0)
    widen = (source == label).astype(F32).astype(BF16)
    target = lax.broadcasted_iota(jnp.int32, (8, NK), 0) + mom * KB
    pick = (target == lax.broadcasted_iota(jnp.int32, (8, NK), 1)).astype(F32).astype(BF16)
    table = idx_ref[...].astype(F32).astype(BF16)
    table = jnp.dot(pick, table, preferred_element_type=F32).astype(BF16)
    table = jnp.dot(table, widen, preferred_element_type=F32)
    mode = lax.broadcasted_iota(jnp.int32, (NW, DEPTH), 0)
    occ = jnp.zeros((NW, DEPTH), F32)
    off = jnp.zeros((NW, DEPTH), jnp.int32)
    for w in range(NW):
        occ = jnp.where(mode == w, occ_ref[w], occ)
        off = jnp.where(mode == w, off_ref[w], off)
    place_of = lax.broadcasted_iota(jnp.int32, (NW, DEPTH), 1)
    pair_of = lax.div(place_of, CHIPS * ROWS)
    energy_of = 2 * (pair_of - 1) + lax.div(lax.rem(place_of, ROWS), 8)
    first = (energy > 0).astype(F32)
    last = (energy < energies - 1).astype(F32)
    values = [[] for _ in range(2)]
    for k in range(KB):
        chosen = (table[k : k + 1, :] == label.astype(F32)).astype(F32).astype(BF16)
        spread = jnp.dot(tc_ref[...], chosen, preferred_element_type=F32)
        low = (occ * spread).astype(BF16).astype(F32)
        high = ((occ + 1.0) * spread).astype(BF16).astype(F32)
        for e in range(2):
            away = energy_of - e
            value = jnp.where(away < 0, low, high)
            values[e].append(jnp.where(jnp.abs(away) == off, value, 0.0))
    value = jnp.concatenate(values[0] + values[1], axis=0)
    pair_of = lax.div(lax.broadcasted_iota(jnp.int32, (TGT, DEPTH), 1), CHIPS * ROWS)
    for t, kept in ((0, first), (1, None), (2, last)):
        now = value if kept is None else jnp.where(pair_of == t, value * kept, value)
        weights[t] = now.astype(BF16)
        above = jnp.zeros((SHIFT, DEPTH), F32)
        below = jnp.zeros((ODD - TGT - SHIFT, DEPTH), F32)
        odd_weights[t] = jnp.concatenate([above, now, below], axis=0).astype(BF16)

    here = lax.broadcasted_iota(jnp.int32, (128, 128), 1)
    row = lax.rem(here, PART)
    wanted = lax.div(lax.rem(here, 2 * PART), PART) * NO + lax.div(here, 2 * PART) * CHUNK
    wanted = wanted + lax.div(row, CHUNK) * HALF + lax.rem(row, CHUNK)
    apart = (wanted == lax.broadcasted_iota(jnp.int32, (128, 128), 0)).astype(F32).astype(BF16)
    right_mats[...] = jnp.zeros_like(right_mats)
    for i in range(NW // 2):
        moved = []
        for h in range(2):
            real = orb_ref[2 * i + h, 0].astype(F32)
            imag = orb_ref[2 * i + h, 1].astype(F32)
            top = jnp.concatenate([real, imag], axis=1)
            bottom = jnp.concatenate([-imag, real], axis=1)
            block = jnp.concatenate([top, bottom], axis=0).T.astype(BF16)
            right_mats[i, pl.ds(h * 128, 128), pl.ds(h * 128, 128)] = block
            moved.append(jnp.dot(top.astype(BF16), apart, preferred_element_type=F32))
        for part in range(2):
            columns = slice(part * 2 * PART, (part + 1) * 2 * PART)
            pair = jnp.concatenate([m[:, columns] for m in moved], axis=1)
            left_mats[part, :, pl.ds(i * 128, 128)] = pair.astype(BF16)

    def mix(side, chunk):
        base = side * HALF + chunk * CHUNK

        def one(t, carry):
            for i in range(CHUNK // 4):
                for odd, matrix in enumerate((weights, odd_weights)):
                    wide = []
                    for r in (4 * i + odd, 4 * i + odd + 2):
                        parts = [buf[t + p, s, base + r] for p in range(3) for s in range(CHIPS)]
                        wide.append(jnp.concatenate(parts, axis=0))
                    got = jnp.dot(
                        matrix[t], jnp.concatenate(wide, axis=1), preferred_element_type=F32
                    )
                    start = (t * PART + side * CHUNK + 4 * i) * MIXSTEP + odd * (MIXSTEP - SHIFT)
                    mixed[pl.ds(pl.multiple_of(start, 8), matrix.shape[1]), :] = got[:, :128]
                    start = start + 2 * MIXSTEP
                    mixed[pl.ds(pl.multiple_of(start, 8), matrix.shape[1]), :] = got[:, 128:]
            return carry

        lax.fori_loop(0, 3, one, 0)

    def modes(part, t):
        for i in range(NW // 2):
            pair = []
            for w in (2 * i, 2 * i + 1):
                rows = []
                for n in range(2 * KB):
                    start = t * (PART * MIXSTEP) + n * NW + w
                    rows.append(mixed[pl.ds(start, PART, stride=MIXSTEP), :].astype(BF16))
                pair.append(jnp.concatenate(rows, axis=0))
            got = jnp.dot(
                jnp.concatenate(pair, axis=1), right_mats[i], preferred_element_type=F32
            ).astype(BF16)
            for h in range(2):
                depth = (2 * i + h) * 2 * PART
                y = got[:, h * 128 : (h + 1) * 128]
                turned = jnp.concatenate([-y[:, NO:], y[:, :NO]], axis=1)
                for n in range(2 * KB):
                    rows = slice(n * PART, (n + 1) * PART)
                    sides[n, pl.ds(depth, PART), :] = y[rows]
                    sides[n, pl.ds(depth + PART, PART), :] = turned[rows]
        for j in range(KB):
            both = jnp.concatenate([sides[2 * j], sides[2 * j + 1]], axis=1)
            got = jnp.dot(left_mats[part], both, preferred_element_type=F32)
            for h in range(2):
                rows = pl.ds(pl.multiple_of(t * OUT + (2 * j + h) * NO, NO), NO)
                value = got[:, h * 128 : (h + 1) * 128]
                if part == 0:
                    out_ref[rows, :] = value
                else:
                    out_ref[rows, :] += value

    now = late + LAG
    steps(EARLY, now)
    on_each_chip(
        lambda place: receive(place, [c for row in incoming[place] for c in row if c[1] == 0])
    )
    mix(core, 0)
    steps(now, now + 1)
    from_sibling(0)
    mix(1 - core, 0)
    steps(now + 1, now + 2)
    for t in range(3):
        modes(0, t)
        steps(now + 2 + t, now + 3 + t)
    steps(now + 5, STEPS + max(CAP, LAG))
    mix(core, 1)
    from_sibling(1)
    mix(1 - core, 1)

    def second(t, carry):
        modes(1, t)
        return carry

    lax.fori_loop(0, 3, second, 0)

    raw_copy(core).wait_send()

    def finish(place):
        for slot in [(p, s) for p in range(PAIRS) for s in range(CHIPS)]:
            for chunk in range(2):
                sib_copy(slot, chunk, core).wait_send()

    finish(0)


def body(green, occupation, coupling, orbital, offsets, index):
    hbm = pl.BlockSpec(memory_space=pltpu.HBM)
    operands = [
        pltpu.with_memory_space_constraint(a, pltpu.HBM)
        for a in (green, occupation, offsets, coupling, index, orbital)
    ]
    slots = PAIRS * CHIPS * 2
    result = pl.pallas_call(
        kernel,
        out_shape=jax.ShapeDtypeStruct((3 * OUT, 128), F32),
        in_specs=[hbm] * 6,
        out_specs=pl.BlockSpec(memory_space=pltpu.VMEM),
        scratch_shapes=[
            pltpu.VMEM((2, EB, KB, HALF, 128), BF16),
            pltpu.VMEM((3 * ROWS * RAWSTEP + 40, 128), F32),
            pltpu.VMEM((PAIRS, CHIPS, NO, ROWS, 128), BF16),
            pltpu.VMEM((3, TGT, DEPTH), BF16),
            pltpu.VMEM((3, ODD, DEPTH), BF16),
            pltpu.VMEM((2, NO, NW * 2 * PART), BF16),
            pltpu.VMEM((NW // 2, 256, 256), BF16),
            pltpu.VMEM(((3 * PART + 2) * MIXSTEP, 128), F32),
            pltpu.VMEM((2 * KB, NW * 2 * PART, 128), BF16),
            pltpu.SMEM((NW,), F32),
            pltpu.SMEM((NW,), jnp.int32),
            pltpu.VMEM((NW, NK), BF16),
            pltpu.VMEM((NK, NK), jnp.int32),
            pltpu.VMEM((NW, 2, NO, NO), BF16),
            pltpu.SemaphoreType.DMA((5,)),
            pltpu.SemaphoreType.DMA,
            pltpu.SemaphoreType.DMA,
            pltpu.SemaphoreType.DMA,
            pltpu.SemaphoreType.DMA((2, CAP)),
            pltpu.SemaphoreType.DMA((slots,)),
            pltpu.SemaphoreType.DMA((slots,)),
            pltpu.SemaphoreType.DMA((slots,)),
        ],
        compiler_params=pltpu.CompilerParams(
            collective_id=0, has_side_effects=True, vmem_limit_bytes=48 * 1024 * 1024
        ),
    )(*operands)
    return result.reshape(green.shape)


def solution(mesh):
    placed = (P("energy", "mom", None, None), P(), P(), P(), P(), P())
    return jax.shard_map(
        body, mesh=mesh, in_specs=placed, out_specs=P("energy", "mom", None, None), check_vma=False
    )
```
